256 devices in a mesh: tp: 8 (over y, core), dp: 32 (over z, x).
Axes of the slice: x: 4, y: 4, z: 8, core: 2. Of those that a mesh axis runs over, the one named last changes fastest.
Arguments:
- queries: bfloat16 [64, 8, 4, 8192], P('dp', None, None, 'tp'), may hold values from -100 to 100
- new_keys: bfloat16 [64, 8, 4, 1024], P('dp', None, None, 'tp'), may hold values from -12 to 12
- new_values: bfloat16 [64, 8, 4, 1024], P('dp', None, None, 'tp'), may hold values from -6 to 6
- key_pool: bfloat16 [5120, 64, 1024], P('dp', None, 'tp'), may hold values from -6 to 6
- value_pool: bfloat16 [5120, 64, 1024], P('dp', None, 'tp'), may hold values from -6 to 6
- out_weight: bfloat16 [8192, 8192], P('tp', 'dp'), may hold values from -0.0625 to 0.0625
- mem_len: int32 [64], replicated, may hold values from 426 to 5120, as said below
- assign: int32 [64], replicated, may hold values from 0 to 63, as said below
- block_table: int32 [64, 80], replicated, may hold values from 0 to 5119, as said below
Outputs:
- layer_out: bfloat16 [2048, 8192], P('tp', 'dp')
- decode_keys: bfloat16 [64, 5120, 1024], P('dp', None, 'tp')
- decode_values: bfloat16 [64, 5120, 1024], P('dp', None, 'tp')
The draws below stay inside these ranges and needn't reach their ends.
Inputs may be any that keep to these rules, and one draw needn't show every extreme that they name: `mem_len`: some prompt's memory is exactly 5120 tokens long. `assign`: A permutation of the prompts; the slots of index d of dp are 2 * d to 2 * d + 1. `block_table`: page id g lies on index g // 160 of dp, at local page g % 160. Every page id appears exactly once in the table. For every pair of indices d and e of dp, exactly 5 of the table entries of the prompts in the slots of d lie on e. Entries past a prompt's memory are valid ids whose contents are not used.
All inputs are finite; a program needn't handle non-finite values.
Results may differ from the reference program's by a relative error of at most 0.019.
Values may be sent and summed in bfloat16 or wider, within the bound.
A program may use at most 64 MiB of HBM per device.

```python
import math
import jax
import jax.numpy as jnp
from jax import lax

D = 8192
HD = 128
KVH = 8
QPK = 8
PAGE = 64
MAX_PAGES = 80
REQ_DEV = 2
SAMPLES = 8
STEPS = 4
SLOTS = 64
POOL = 160
CAP = 5
MIN_LEN = 426
N_DP = 32


def plan_tables(key):
    key_assign, key_cells, key_local = jax.random.split(key, 3)
    assign = jax.random.permutation(key_assign, SLOTS).astype(jnp.int32)
    entry_count = REQ_DEV * MAX_PAGES
    cell_ids = jax.vmap(lambda subkey: jax.random.permutation(subkey, entry_count))(jax.random.split(key_cells, N_DP)).astype(jnp.int32)
    source = cell_ids // CAP
    within = cell_ids % CAP
    local_orders = jax.vmap(lambda subkey: jax.random.permutation(subkey, POOL))(jax.random.split(key_local, N_DP)).astype(jnp.int32)
    target = jnp.arange(N_DP, dtype=jnp.int32)[:, None] * CAP + within
    local_page = local_orders[source, target]
    global_page = source * POOL + local_page
    slot_tables = global_page.reshape(SLOTS, MAX_PAGES)
    page_table = jnp.zeros((SLOTS, MAX_PAGES), jnp.int32).at[assign].set(slot_tables)
    return (assign, page_table)


def draw_assign(key, part):
    return plan_tables(key)[0]


def draw_block_table(key, part):
    return plan_tables(key)[1]


def draw_mem_len(key, part):
    key = jax.random.fold_in(key, 7)
    key_len, key_top = jax.random.split(key)
    drawn = jax.random.randint(key_len, (SLOTS,), 0, 1025)
    squared = drawn * drawn // 1024
    lengths = MIN_LEN + (MAX_PAGES * PAGE - MIN_LEN) * squared // 1024
    longest = jax.random.randint(key_top, (), 0, SLOTS)
    lengths = jnp.where(jnp.arange(SLOTS, dtype=jnp.int32) == longest, MAX_PAGES * PAGE, lengths)
    return lengths.astype(jnp.int32)


def draw_queries(key, part):
    key = jax.random.fold_in(key, 11)
    entries = jnp.clip(jax.random.normal(key, (SLOTS, SAMPLES, STEPS, KVH, QPK, HD), jnp.float32), -6.0, 6.0)
    return entries.reshape(SLOTS, SAMPLES, STEPS, KVH * QPK * HD).astype(jnp.bfloat16)


def draw_new_keys(key, part):
    key = jax.random.fold_in(key, 13)
    entries = jnp.clip(jax.random.normal(key, (SLOTS, SAMPLES, STEPS, KVH, HD), jnp.float32), -6.0, 6.0)
    return entries.reshape(SLOTS, SAMPLES, STEPS, KVH * HD).astype(jnp.bfloat16)


def levels(rng, shape, shards, smallest, largest):
    level, own = 1.0, jax.random.fold_in(rng, 6)
    for dim, parts in shards:
        draws = jnp.exp(jax.random.uniform(jax.random.fold_in(own, dim), (parts,), jnp.float32, smallest / len(shards), largest / len(shards)))
        level = level * jnp.repeat(draws, shape[dim] // parts).reshape([-1 if axis == dim else 1 for axis in range(len(shape))])
    return level


def normal_values(own_key, shape, deviation, reach, cuts=(), held_as=jnp.bfloat16):
    level = levels(own_key, shape, cuts, -0.22, 0.18) if cuts else 1.0
    array = jax.random.normal(own_key, shape, jnp.float32) * deviation * level
    return jnp.minimum(jnp.maximum(array, -reach), reach).astype(held_as)


def setup_inputs(seed: int = 0) -> dict:
    key_of = jax.random.split(jax.random.key(seed), 10)
    return {
        "queries": draw_queries(jax.random.fold_in(key_of[9], 71), 0),
        "new_keys": draw_new_keys(jax.random.fold_in(key_of[9], 71), 0),
        "new_values": normal_values(key_of[2], (SLOTS, SAMPLES, STEPS, KVH * HD), 1.0, 6.0, ((0, 32), (3, 8))),
        "key_pool": normal_values(key_of[3], (N_DP * POOL, PAGE, KVH * HD), 1.0, 6.0, ((0, 32), (2, 8))),
        "value_pool": normal_values(key_of[4], (N_DP * POOL, PAGE, KVH * HD), 1.0, 6.0, ((0, 32), (2, 8))),
        "out_weight": normal_values(key_of[5], (KVH * QPK * HD, D), (KVH * QPK * HD) ** -0.5, 0.0625, ((0, 8), (1, 32))),
        "mem_len": draw_mem_len(jax.random.fold_in(key_of[9], 71), 0),
        "assign": draw_assign(jax.random.fold_in(key_of[9], 71), 0),
        "block_table": draw_block_table(jax.random.fold_in(key_of[9], 71), 0),
    }


def slot_output(query, memory_keys, memory_values, fresh_keys, fresh_values, length):
    sample_count = query.shape[0]
    step_count = query.shape[1]
    kv_heads = memory_keys.shape[1] // HD
    score_scale = 1.0 / math.sqrt(HD)
    query_heads = query.astype(jnp.float32).reshape(sample_count, step_count, kv_heads, QPK, HD)
    key_heads = memory_keys.astype(jnp.float32).reshape(-1, kv_heads, HD)
    value_heads = memory_values.astype(jnp.float32).reshape(-1, kv_heads, HD)
    fresh_key_heads = fresh_keys.astype(jnp.float32).reshape(sample_count, step_count, kv_heads, HD)
    fresh_value_heads = fresh_values.astype(jnp.float32).reshape(sample_count, step_count, kv_heads, HD)
    memory_scores = jnp.einsum('ashgd,khd->ashgk', query_heads, key_heads) * score_scale
    usable = jnp.arange(key_heads.shape[0], dtype=jnp.int32) < length
    memory_scores = jnp.where(usable[None, None, None, None, :], memory_scores, -jnp.inf)
    fresh_scores = jnp.einsum('ashgd,auhd->ashgu', query_heads, fresh_key_heads) * score_scale
    causal = jnp.arange(step_count)[:, None] >= jnp.arange(step_count)[None, :]
    fresh_scores = jnp.where(causal[None, :, None, None, :], fresh_scores, -jnp.inf)
    row_max = jnp.maximum(lax.optimization_barrier(jnp.max(memory_scores, axis=-1)), lax.optimization_barrier(jnp.max(fresh_scores, axis=-1)))
    memory_weights = jnp.exp(memory_scores - row_max[..., None])
    fresh_weights = jnp.exp(fresh_scores - row_max[..., None])
    row_total = lax.optimization_barrier(jnp.sum(memory_weights, axis=-1)) + lax.optimization_barrier(jnp.sum(fresh_weights, axis=-1))
    memory_low = memory_weights.astype(jnp.bfloat16).astype(jnp.float32)
    fresh_low = fresh_weights.astype(jnp.bfloat16).astype(jnp.float32)
    weighted = jnp.einsum('ashgk,khd->ashgd', memory_low, value_heads)
    weighted = weighted + jnp.einsum('ashgu,auhd->ashgd', fresh_low, fresh_value_heads)
    mixed = weighted / row_total[..., None]
    return mixed.reshape(sample_count * step_count, -1).astype(jnp.bfloat16)

def reference(queries, new_keys, new_values, key_pool, value_pool, out_weight, mem_len, assign, block_table):

    def one_slot(slot):
        prompt = assign[slot]
        page_ids = block_table[prompt]
        length = mem_len[prompt]
        memory_keys = key_pool[page_ids].reshape(MAX_PAGES * PAGE, -1)
        memory_values = value_pool[page_ids].reshape(MAX_PAGES * PAGE, -1)
        usable = (jnp.arange(MAX_PAGES * PAGE, dtype=jnp.int32) < length)[:, None]
        memory_keys = jnp.where(usable, memory_keys, jnp.zeros_like(memory_keys))
        memory_values = jnp.where(usable, memory_values, jnp.zeros_like(memory_values))
        slot_mixed = slot_output(queries[slot], memory_keys, memory_values, new_keys[slot], new_values[slot], length)
        return (slot_mixed, memory_keys, memory_values)
    attention, decode_keys, decode_values = lax.map(one_slot, jnp.arange(SLOTS, dtype=jnp.int32))
    attention_rows = attention.reshape(SLOTS * SAMPLES * STEPS, -1)
    layer_out = jnp.dot(attention_rows, out_weight, preferred_element_type=jnp.float32).astype(jnp.bfloat16)
    return (layer_out, decode_keys, decode_values)
```

```python
import functools
import math

import jax
import jax.numpy as jnp
from jax import lax
from jax.experimental import pallas as pl
from jax.experimental.pallas import tpu as pltpu
from jax.sharding import PartitionSpec as P

MESH = pl.DeviceIdType.MESH
BF = jnp.bfloat16
F32 = jnp.float32
I32 = jnp.int32

NZ, NX, NT = 8, 4, 8
HD = 128
QPK = 8
PAGE = 64
PAGES = 80
POOL = 160
SPAN = PAGES * PAGE

FULL = (70, 50, 30, 10)
XFULL = 40
LEVELS = (
    ((38, 29, 19, 8), 38),
    ((44, 33, 23, 9), 40),
    (FULL, XFULL),
)
OWN = 20
PLUS = (20, 90, 140, 170)
MINUS = (180, 250, 300, 330)
ZROOM = 340
SEND_MINUS = 70
CHUNKS = ((0, 0, 32), (0, 32, 32), (1, 0, 32), (1, 32, 16), (1, 48, 16))


def dot(a, b, dims, precision=None):
    return lax.dot_general(a, b, (dims, ((), ())), precision=precision, preferred_element_type=F32)


def tables_kernel(len_ref, assign_ref, bt_ref, t3_ref, t12_ref, lens_ref, level_ref, raw, longs, src_s, used_s, list_s):
    me = lax.axis_index("dp")
    z, x = me // NX, me % NX
    raw[...] = jnp.zeros_like(raw)
    for s in range(64):
        a = assign_ref[s]
        raw[s : s + 1, 0:PAGES] = bt_ref[pl.ds(a, 1), :]
        longs[s : s + 1, :] = jnp.full((1, 128), len_ref[a], I32)

    shape = (64, 128)
    slot = lax.broadcasted_iota(I32, shape, 0)
    lane = lax.broadcasted_iota(I32, shape, 1)
    page = raw[...]
    src = (page * 26215) >> 22
    loc = (page - src * POOL).astype(F32)
    used = jnp.where((lane < PAGES) & (lane * PAGE < longs[...]), 1, 0)
    src = jnp.where(used == 1, src, 1000)
    src_s[...] = src

    tri = jnp.where(lax.broadcasted_iota(I32, (128, 128), 0) < lax.broadcasted_iota(I32, (128, 128), 1), 1.0, 0.0).astype(BF)
    bi, bj = lax.broadcasted_iota(I32, (64, 64), 0), lax.broadcasted_iota(I32, (64, 64), 1)
    blocks = jnp.where((bi // 8 == bj // 8) & (bj < bi), 1.0, 0.0).astype(BF)

    def ranks(mask):
        total = jnp.broadcast_to(jnp.sum(mask, axis=1, keepdims=True), shape)
        return dot(mask.astype(BF), tri, ((1,), (0,))) + dot(blocks, total.astype(BF), ((1,), (0,)))

    count = jnp.zeros(shape, F32)
    for e in range(32):
        total = jnp.sum(jnp.where(src == e, 1.0, 0.0), axis=1, keepdims=True)
        count = jnp.where(lane == e, total, count)
    dist = (slot // 8 - lane // NX) & 7
    at = [jnp.sum(jnp.where((dist == k) & (lane < 32), count, 0.0), axis=0, keepdims=True) for k in range(8)]
    p4 = jnp.floor((at[4] + 1.0) * 0.5)
    m4 = at[4] - p4
    plus = [None] * 5
    minus = [None] * 5
    plus[4], minus[4] = p4, m4
    for j in (3, 2, 1):
        plus[j] = plus[j + 1] + at[j]
        minus[j] = minus[j + 1] + at[8 - j]
    nil = jnp.zeros_like(p4)
    offset = [nil, plus[2], plus[3], plus[4], nil, minus[4], minus[3], minus[2]]

    by_x = jnp.zeros(shape, F32)
    for k in range(NX):
        total = jnp.sum(jnp.where((lane & 3) == k, count, 0.0), axis=1, keepdims=True)
        by_x = jnp.where(lane == k, total, by_x)
    pairs = by_x + pltpu.roll(by_x, 1, 0)
    pairs = jnp.where((slot % 2 == 1) & (lane != (slot // 2) % NX), pairs, 0.0)
    x_most = jnp.max(pairs)
    needs = [(jnp.maximum(jnp.max(plus[j]), jnp.max(minus[j])), j - 1) for j in (1, 2, 3, 4)]
    level = jnp.int32(0)
    for caps, x_cap in LEVELS[:-1]:
        over = jnp.where(x_most > float(x_cap), 1, 0)
        for need, j in needs:
            over = jnp.maximum(over, jnp.where(need > float(caps[j]), 1, 0))
        level = level + over
    level_ref[0] = level

    def column(row, e):
        return jnp.sum(jnp.where(lax.broadcasted_iota(I32, (1, 128), 1) == e, row, 0.0), axis=1, keepdims=True)

    mine = src == me
    rank = ranks(jnp.where(mine, 1.0, 0.0))
    away = (slot // 8 - z) & 7
    half = column(p4, me)
    place = rank
    for k in range(1, 8):
        base = OWN if k < 4 else OWN + SEND_MINUS
        value = column(offset[k], me) + rank + float(base)
        if k == 4:
            value = jnp.where(rank < half, rank + float(OWN), rank - half + float(OWN + SEND_MINUS))
        place = jnp.where(away == k, value, place)
    place = jnp.where(mine, place, -1.0)

    def first_list(g, _):
        rows = []
        for i in range(8):
            k = (g * 8 + i).astype(F32)
            rows.append(jnp.sum(jnp.where(place == k, loc, 0.0), axis=0, keepdims=True))
        list_s[pl.ds(pl.multiple_of(g * 8, 8), 8), :] = jnp.concatenate(rows, axis=0)
        return 0

    lax.fori_loop(0, 20, first_list, 0)
    ones = jnp.ones((8, 128), F32)
    t12_ref[0:8, :] = dot(ones, list_s[...], ((1,), (1,)), lax.Precision.HIGHEST).astype(I32)

    row8 = pl.ds(pl.multiple_of(z * 8, 8), 8)
    src_r = src_s[row8, :]
    marks = jnp.concatenate([jnp.where(src_r == zs * NX + x, 1.0, 0.0) for zs in range(NZ)], axis=0)
    rank = ranks(marks)
    off8 = jnp.concatenate(offset, axis=0)
    k8 = lax.broadcasted_iota(I32, (8, 128), 0)
    e8 = lax.broadcasted_iota(I32, (8, 128), 1)
    here = (e8 & 3) == x
    off_e = jnp.sum(jnp.where(here & (k8 == ((z - e8 // NX) & 7)), off8, 0.0), axis=0, keepdims=True)
    half_e = jnp.where(here[0:1], p4, 0.0)
    through = jnp.zeros((8, 128), F32)
    for zs in range(NZ):
        r = rank[zs * 8 : zs * 8 + 8]
        pick = (e8[0:1] // NX) == zs
        off = jnp.sum(jnp.where(pick, off_e, 0.0), axis=1, keepdims=True)
        half = jnp.sum(jnp.where(pick, half_e, 0.0), axis=1, keepdims=True)
        d = jnp.broadcast_to((z - zs) & 7, (8, 128))
        value = r
        for k in range(1, 8):
            if k == 4:
                v = jnp.where(r < half, r + float(PLUS[3]), r - half + float(MINUS[3]))
            else:
                v = off + r + float(PLUS[k - 1] if k < 4 else MINUS[7 - k])
            value = jnp.where(d == k, v, value)
        through = through + marks[zs * 8 : zs * 8 + 8] * value

    used_r = src_r < 32
    odd = (k8 & 1) == 1
    order = jnp.zeros((8, 128), F32)
    for k in range(NX):
        mark = jnp.where(used_r & ((src_r & 3) == k), 1.0, 0.0)
        total = jnp.broadcast_to(jnp.sum(mark, axis=1, keepdims=True), (8, 128))
        r = dot(mark.astype(BF), tri, ((1,), (0,))) + jnp.where(odd, pltpu.roll(total, 1, 0), 0.0)
        order = order + mark * r
    order_i = order.astype(I32)
    t3_ref[...] = jnp.where(used_r, ((src_r - x) & 3) * XFULL + order_i, 0)
    lens_ref[...] = longs[row8, :]
    goes = ((k8 // 2 - x) & 3) * XFULL + order_i
    goes = jnp.where(used_r & ((src_r & 3) == x), goes, -1)

    def second_list(g, _):
        rows = []
        for i in range(8):
            rows.append(jnp.sum(jnp.where(goes == g * 8 + i, through, 0.0), axis=0, keepdims=True))
        list_s[pl.ds(pl.multiple_of(g * 8, 8), 8), :] = jnp.concatenate(rows, axis=0)
        return 0

    lax.fori_loop(0, 20, second_list, 0)
    t12_ref[8:16, :] = dot(ones, list_s[...], ((1,), (1,)), lax.Precision.HIGHEST).astype(I32)


def make_tables(mem_len, assign, block_table):
    smem = pl.BlockSpec(memory_space=pltpu.SMEM)
    vmem = pl.BlockSpec(memory_space=pltpu.VMEM)
    return pl.pallas_call(
        tables_kernel,
        out_shape=(
            jax.ShapeDtypeStruct((8, 128), I32),
            jax.ShapeDtypeStruct((16, 160), I32),
            jax.ShapeDtypeStruct((8, 128), I32),
            jax.ShapeDtypeStruct((1,), I32),
        ),
        in_specs=[smem, smem, vmem],
        out_specs=(vmem, vmem, vmem, smem),
        scratch_shapes=[
            pltpu.VMEM((64, 128), I32),
            pltpu.VMEM((64, 128), I32),
            pltpu.VMEM((64, 128), I32),
            pltpu.VMEM((64, 128), I32),
            pltpu.VMEM((160, 128), F32),
        ],
    )(mem_len, assign, block_table)


def handoff_kernel(caps, x_cap, *refs):
    n = len(CHUNKS)
    it = iter(refs)
    t3, t12, lens, q_ref, nk_ref, nv_ref, kp_hbm, vp_hbm, w_hbm = (next(it) for _ in range(9))
    lo_ref, ko_hbm, vo_hbm = (next(it) for _ in range(3))
    pools = (next(it), next(it))
    staged = (next(it), next(it))
    zs = [next(it) for _ in range(n)]
    zb = [next(it) for _ in range(n)]
    xs = [next(it) for _ in range(n)]
    xb = [next(it) for _ in range(n)]
    probs, att, wbuf, abuf, part, rbuf, fin_s, fin = (next(it) for _ in range(8))
    local_sem, z_send, z_recv, x_send, x_recv, w_send, w_recv, a_send, a_recv, r_send, r_recv, f_send, f_recv = it

    me, tp = lax.axis_index("dp"), lax.axis_index("tp")
    z, x = me // NX, me % NX
    z_to = [{"dp": ((z + 1) % NZ) * NX + x}, {"dp": ((z + NZ - 1) % NZ) * NX + x}]
    x_to = [{"dp": z * NX + (x + r) % NX} for r in range(NX)]
    t_to = [{"tp": (tp + r) % NT} for r in range(NT)]

    loads = [
        pltpu.make_async_copy(kp_hbm, pools[0], local_sem.at[0]),
        pltpu.make_async_copy(vp_hbm, pools[1], local_sem.at[1]),
        pltpu.make_async_copy(w_hbm, wbuf.at[0], local_sem.at[2]),
    ]
    for c in loads:
        c.start()
    barrier = pltpu.get_barrier_semaphore()
    peers = z_to + x_to[1:] + t_to[1:]
    for d in peers:
        pl.semaphore_signal(barrier, inc=1, device_id=d, device_id_type=MESH)

    def remote(src, dst, ss, rs, to):
        return pltpu.make_async_remote_copy(
            src_ref=src, dst_ref=dst, send_sem=ss, recv_sem=rs, device_id=to, device_id_type=MESH
        )

    sent = []

    def z_copy(c, d, j):
        base = (PLUS, MINUS)[d]
        if j == 1:
            src = zs[c].at[pl.ds(d * SEND_MINUS, caps[0])]
        else:
            src = zb[c].at[pl.ds(base[j - 2], caps[j - 1])]
        return remote(src, zb[c].at[pl.ds(base[j - 1], caps[j - 1])], z_send.at[c, d, j - 1], z_recv.at[c, d, j - 1], z_to[d])

    def z_start(c, j):
        for d in range(2):
            cp = z_copy(c, d, j)
            cp.start()
            sent.append(cp)

    def x_copy(c, r):
        return remote(
            xs[c].at[pl.ds((r - 1) * XFULL, x_cap)],
            xb[c].at[pl.ds((NX - r) * XFULL, x_cap)],
            x_send.at[c, r - 1],
            x_recv.at[c, r - 1],
            x_to[r],
        )

    def pack_pool(which):
        mine = [(c, r0, rows) for c, (w, r0, rows) in enumerate(CHUNKS) if w == which]
        pool = pools[which]

        def body(first, dst, place, k, _):
            got = pool[t12[0, first + k]]
            for c, r0, rows in mine:
                dst[c][place + k] = got[r0 : r0 + rows]
            return 0

        lax.fori_loop(0, OWN, functools.partial(body, 0, zb, 0), 0, unroll=4)
        lax.fori_loop(0, caps[0], functools.partial(body, OWN, zs, 0), 0, unroll=2)
        lax.fori_loop(0, caps[0], functools.partial(body, OWN + SEND_MINUS, zs, SEND_MINUS), 0, unroll=2)

    def pack_row(c):
        def body(first, dst, place, k, _):
            dst[place + k] = zb[c][t12[8, first + k]]
            return 0

        for r in (2, 1, 3):
            lax.fori_loop(0, x_cap, functools.partial(body, r * XFULL, xs[c], (r - 1) * XFULL), 0, unroll=2)
            cp = x_copy(c, r)
            cp.start()
            sent.append(cp)
        lax.fori_loop(0, XFULL, functools.partial(body, 0, xb[c], 0), 0, unroll=4)

    def place_pages(c):
        which, r0, rows = CHUNKS[c]
        token = lax.broadcasted_iota(I32, (rows, HD), 0)
        for s in range(2):

            def body(p, _):
                got = xb[c][t3[2 * x + s, p]]
                left = lens[2 * x + s, 0] - p * PAGE - r0
                got = jnp.where(token < left, got.astype(F32), 0.0).astype(BF)
                staged[which][s, pl.ds(pl.multiple_of(p * PAGE + r0, 16), rows), :] = got
                return 0

            lax.fori_loop(0, PAGES, body, 0, unroll=4)

    scale = 1.0 / math.sqrt(HD)
    tile = 512

    def queries_of(s):
        rows = q_ref[s * 32 : (s + 1) * 32, :]
        return jnp.concatenate([rows[:, h * HD : (h + 1) * HD] for h in range(QPK)], axis=0)

    def fresh_scores(s):
        sc = dot(queries_of(s), nk_ref[s * 32 : (s + 1) * 32, :], ((1,), (1,))) * scale
        r = lax.broadcasted_iota(I32, sc.shape, 0) % 32
        u = lax.broadcasted_iota(I32, sc.shape, 1)
        ok = (r // 4 == u // 4) & (u % 4 <= r % 4)
        return jnp.where(ok, sc, -jnp.inf)

    def tile_scores(s, q, i, length):
        keys = staged[0][s, pl.ds(pl.multiple_of(i * tile, tile), tile), :]
        sc = dot(q, keys, ((1,), (1,))) * scale
        pos = lax.broadcasted_iota(I32, sc.shape, 1) + i * tile
        return jnp.where(pos < length, sc, -jnp.inf)

    def find_max(s):
        q = queries_of(s)
        length = lens[2 * x + s, 0]

        def body(i, m):
            sc = tile_scores(s, q, i, length)
            for k in range(tile // 128):
                m = jnp.maximum(m, sc[:, k * 128 : (k + 1) * 128])
            return m

        m = lax.fori_loop(0, SPAN // tile, body, jnp.full((256, 128), -jnp.inf, F32))
        top = jnp.maximum(jnp.max(m, axis=1, keepdims=True), jnp.max(fresh_scores(s), axis=1, keepdims=True))
        att[s, 0] = jnp.broadcast_to(top, (256, 128))

    def weigh(s):
        q = queries_of(s)
        length = lens[2 * x + s, 0]
        top = att[s, 0][:, 0:1]

        def body(i, t):
            w = jnp.exp(tile_scores(s, q, i, length) - top)
            probs[s, :, pl.ds(pl.multiple_of(i * tile, tile), tile)] = w.astype(BF)
            for k in range(tile // 128):
                t = t + w[:, k * 128 : (k + 1) * 128]
            return t

        t = lax.fori_loop(0, SPAN // tile, body, jnp.zeros((256, 128), F32))
        fresh = jnp.exp(fresh_scores(s) - top)
        total = jnp.sum(t, axis=1, keepdims=True) + jnp.sum(fresh, axis=1, keepdims=True)
        att[s, 0] = jnp.broadcast_to(total, (256, 128))
        att[s, 1] = dot(fresh.astype(BF), nv_ref[s * 32 : (s + 1) * 32, :], ((1,), (0,)))

    def finish(s):
        acc = att[s, 1]

        def body(i, a):
            at = pl.ds(pl.multiple_of(i * 1024, 1024), 1024)
            return a + dot(probs[s, :, at], staged[1][s, at, :], ((1,), (0,)))

        acc = lax.fori_loop(0, SPAN // 1024, body, acc)
        rows = (acc / att[s, 0]).astype(BF)
        for h in range(QPK):
            abuf[0, s * 32 : (s + 1) * 32, h * HD : (h + 1) * HD] = rows[h * 32 : (h + 1) * 32, :]

    half = wbuf.shape[1] // 2

    def w_copy(i):
        src, dst, r = (
            (wbuf.at[0], wbuf.at[3], 1),
            (wbuf.at[0], wbuf.at[1], 3),
            (wbuf.at[3, pl.ds(0, half)], wbuf.at[2, pl.ds(0, half)], 1),
            (wbuf.at[1, pl.ds(half, half)], wbuf.at[2, pl.ds(half, half)], 3),
        )[i]
        return remote(src, dst, w_send.at[i], w_recv.at[i], x_to[r])

    def w_start(i):
        cp = w_copy(i)
        cp.start()
        sent.append(cp)

    pl.semaphore_wait(barrier, len(peers))
    loads[0].wait()
    pack_pool(0)
    z_start(0, 1)
    z_start(1, 1)
    loads[2].wait()
    w_start(0)
    w_start(1)
    loads[1].wait()
    pack_pool(1)

    k_last = max(c for c, ch in enumerate(CHUNKS) if ch[0] == 0)
    work = [functools.partial(find_max, 0), functools.partial(find_max, 1), functools.partial(weigh, 0), functools.partial(weigh, 1)]
    flush = []
    k_ready = False
    for r in range(1, n + 6):
        for c in range(max(0, r - 4), min(n, r)):
            j = r - c
            for d in range(2):
                z_copy(c, d, j).wait_recv()
            if j < 4:
                z_start(c, j + 1)
        if r + 1 < n:
            z_start(r + 1, 1)
        if r == 2:
            w_copy(0).wait_recv()
            w_copy(1).wait_recv()
            w_start(2)
            w_start(3)
        if 0 <= r - 4 < n:
            pack_row(r - 4)
        if k_ready and work:
            if r >= n + 3:
                while work:
                    work.pop(0)()
            else:
                work.pop(0)()
        if 0 <= r - 5 < n:
            c = r - 5
            for i in (1, 2, 3):
                x_copy(c, i).wait_recv()
            place_pages(c)
            if c == k_last:
                k_ready = True
                out = pltpu.make_async_copy(staged[0], ko_hbm, local_sem.at[3])
                out.start()
                flush.append(out)
    out = pltpu.make_async_copy(staged[1], vo_hbm, local_sem.at[4])
    out.start()
    flush.append(out)

    def a_copy(s, d, j):
        rows = pl.ds(s * 32, 32)
        here = (j - 1) if d == 0 else (9 - j) % 8
        there = j if d == 0 else 8 - j
        return remote(abuf.at[here, rows], abuf.at[there, rows], a_send.at[s, d, j - 1], a_recv.at[s, d, j - 1], z_to[d])

    def a_start(s, d, j):
        cp = a_copy(s, d, j)
        cp.start()
        sent.append(cp)

    for s in range(2):
        finish(s)
        for d in range(2):
            a_start(s, d, 1)

    w_copy(2).wait_recv()
    w_copy(3).wait_recv()

    def block_copy(r):
        return remote(part.at[r], rbuf.at[tp], r_send.at[r], r_recv.at[tp], {"tp": (z + NZ - r) % NZ})

    def project(r):
        rows = abuf[r]
        for k in range(NX):
            part[r, :, k * 256 : (k + 1) * 256] = dot(rows, wbuf[k], ((1,), (0,))).astype(BF)
        target = (z + NZ - r) % NZ

        @pl.when(target != tp)
        def _():
            block_copy(r).start()

        @pl.when(target == tp)
        def _():
            rbuf[tp] = part[r]

    project(0)
    for j in (1, 2, 3, 4):
        for s in range(2):
            for d in range(2):
                if j < 4 or s == d:
                    a_copy(s, d, j).wait_recv()
                if j < 3 or (j == 3 and s == d):
                    a_start(s, d, j + 1)
        project(j)
        if j < 4:
            project(8 - j)

    total = jnp.zeros((64, 1024), F32)
    for t in range(NT):

        @pl.when(t != tp)
        def _():
            remote(part.at[0], rbuf.at[t], r_send.at[0], r_recv.at[t], t_to[1]).wait_recv()

    for t in range(NT):
        total = total + rbuf[t].astype(F32)
    total = total.astype(BF)
    rows = pl.ds(pl.multiple_of(x * 64, 64), 64)
    fin[rows, :] = total[:, 0:256]
    for k in range(1, NX):
        fin_s[k - 1] = total[:, k * 256 : (k + 1) * 256]
        cp = remote(fin_s.at[k - 1], fin.at[rows], f_send.at[k - 1], f_recv.at[k - 1], x_to[k])
        cp.start()
        sent.append(cp)
    for k in range(1, NX):
        from_rows = pl.ds(pl.multiple_of(((x + NX - k) % NX) * 64, 64), 64)
        remote(fin_s.at[k - 1], fin.at[from_rows], f_send.at[k - 1], f_recv.at[k - 1], x_to[k]).wait_recv()
    lo_ref[...] = fin[...]
    for r in range(NZ):

        @pl.when((z + NZ - r) % NZ != tp)
        def _():
            block_copy(r).wait_send()

    for cp in sent:
        cp.wait_send()
    for cp in flush:
        cp.wait()


def handoff(level, t3, t12, lens, q, nk, nv, key_pool, value_pool, out_weight):
    caps, x_cap = LEVELS[level]
    n = len(CHUNKS)
    smem = pl.BlockSpec(memory_space=pltpu.SMEM)
    vmem = pl.BlockSpec(memory_space=pltpu.VMEM)
    hbm = pl.BlockSpec(memory_space=pl.ANY)
    dma = pltpu.SemaphoreType.DMA
    scratch = [pltpu.VMEM((POOL, PAGE, HD), BF)] * 2 + [pltpu.VMEM((2, SPAN, HD), BF)] * 2
    for pages in (2 * SEND_MINUS, ZROOM, 3 * XFULL, 4 * XFULL):
        scratch += [pltpu.VMEM((pages, rows, HD), BF) for _, _, rows in CHUNKS]
    scratch += [
        pltpu.VMEM((2, 256, SPAN), BF),
        pltpu.VMEM((2, 2, 256, 128), F32),
        pltpu.VMEM((NX, 1024, 256), BF),
        pltpu.VMEM((NZ, 64, 1024), BF),
        pltpu.VMEM((NZ, 64, 1024), BF),
        pltpu.VMEM((NT, 64, 1024), BF),
        pltpu.VMEM((3, 64, 256), BF),
        pltpu.VMEM((256, 256), BF),
        dma((5,)),
        dma((n, 2, 4)),
        dma((n, 2, 4)),
        dma((n, 3)),
        dma((n, 3)),
        dma((4,)),
        dma((4,)),
        dma((2, 2, 4)),
        dma((2, 2, 4)),
        dma((NZ,)),
        dma((NT,)),
        dma((3,)),
        dma((3,)),
    ]
    return pl.pallas_call(
        functools.partial(handoff_kernel, caps, x_cap),
        out_shape=(
            jax.ShapeDtypeStruct((256, 256), BF),
            jax.ShapeDtypeStruct((2, SPAN, HD), BF),
            jax.ShapeDtypeStruct((2, SPAN, HD), BF),
        ),
        in_specs=[smem] * 3 + [vmem] * 3 + [hbm] * 3,
        out_specs=(vmem, hbm, hbm),
        scratch_shapes=scratch,
        compiler_params=pltpu.CompilerParams(
            collective_id=level, has_side_effects=True, vmem_limit_bytes=58 * 2**20
        ),
    )(t3, t12, lens, q, nk, nv, key_pool, value_pool, out_weight)


def local(queries, new_keys, new_values, key_pool, value_pool, out_weight, mem_len, assign, block_table):
    t3, t12, lens, level = make_tables(mem_len, assign, block_table)
    q = queries.reshape(64, 1024)
    nk = new_keys.reshape(64, HD)
    nv = new_values.reshape(64, HD)
    branches = [functools.partial(handoff, i) for i in range(len(LEVELS))]
    return lax.switch(level[0], branches, t3, t12, lens, q, nk, nv, key_pool, value_pool, out_weight)


def solution(mesh):
    placed = (
        P("dp", None, None, "tp"),
        P("dp", None, None, "tp"),
        P("dp", None, None, "tp"),
        P("dp", None, "tp"),
        P("dp", None, "tp"),
        P("tp", "dp"),
        P(),
        P(),
        P(),
    )
    return jax.shard_map(
        local,
        mesh=mesh,
        in_specs=placed,
        out_specs=(P("tp", "dp"), P("dp", None, "tp"), P("dp", None, "tp")),
        check_vma=False,
    )
```

```python
import functools
import math

import jax
import jax.numpy as jnp
from jax import lax
from jax.experimental import pallas as pl
from jax.experimental.pallas import tpu as pltpu
from jax.sharding import PartitionSpec as P

MESH = pl.DeviceIdType.MESH
BF = jnp.bfloat16
F32 = jnp.float32
I32 = jnp.int32

NZ, NX, NT = 8, 4, 8
HD = 128
QPK = 8
PAGE = 64
PAGES = 80
POOL = 160
SPAN = PAGES * PAGE

FULL = (73, 53, 33, 13)
XFULL = 40
LEVELS = (
    (36, 28, 19, 9),
    (39, 30, 21, 10),
    (45, 34, 24, 12),
    FULL,
)
OWN = 20
PLUS = (20, 93, 0, 33)
MINUS = (146, 219, 46, 79)
ZROOM = (272, 92)
XNEAR = 25
SEND_MINUS = FULL[0]
LIST = 168
CHUNKS = tuple((w, r, 16) for w in (0, 1) for r in (0, 16, 32, 48))


def dot(a, b, dims, precision=None):
    return lax.dot_general(a, b, (dims, ((), ())), precision=precision, preferred_element_type=F32)


def tables_kernel(len_ref, assign_ref, bt_ref, t3_ref, t12_ref, lens_ref, level_ref, raw, longs, src_s, used_s, list_s):
    me = lax.axis_index("dp")
    z, x = me // NX, me % NX
    raw[...] = jnp.zeros_like(raw)
    for s in range(64):
        a = assign_ref[s]
        raw[s : s + 1, 0:PAGES] = bt_ref[pl.ds(a, 1), :]
        longs[s : s + 1, :] = jnp.full((1, 128), len_ref[a], I32)

    shape = (64, 128)
    slot = lax.broadcasted_iota(I32, shape, 0)
    lane = lax.broadcasted_iota(I32, shape, 1)
    page = raw[...]
    src = (page * 26215) >> 22
    loc = (page - src * POOL).astype(F32)
    used = jnp.where((lane < PAGES) & (lane * PAGE < longs[...]), 1, 0)
    src = jnp.where(used == 1, src, 1000)
    src_s[...] = src

    tri = jnp.where(lax.broadcasted_iota(I32, (128, 128), 0) < lax.broadcasted_iota(I32, (128, 128), 1), 1.0, 0.0).astype(BF)
    bi, bj = lax.broadcasted_iota(I32, (64, 64), 0), lax.broadcasted_iota(I32, (64, 64), 1)
    blocks = jnp.where((bi // 8 == bj // 8) & (bj < bi), 1.0, 0.0).astype(BF)

    def ranks(mask):
        total = jnp.broadcast_to(jnp.sum(mask, axis=1, keepdims=True), shape)
        return dot(mask.astype(BF), tri, ((1,), (0,))) + dot(blocks, total.astype(BF), ((1,), (0,)))

    count = jnp.zeros(shape, F32)
    for e in range(32):
        total = jnp.sum(jnp.where(src == e, 1.0, 0.0), axis=1, keepdims=True)
        count = jnp.where(lane == e, total, count)
    dist = (slot // 8 - lane // NX) & 7
    at = [jnp.sum(jnp.where((dist == k) & (lane < 32), count, 0.0), axis=0, keepdims=True) for k in range(8)]
    lean = (at[5] + at[6] + at[7] - at[1] - at[2] - at[3]) * 0.25
    middle = at[4] * 0.5
    p4 = jnp.clip(
        jnp.floor(middle + lean + 0.5),
        jnp.floor(jnp.maximum(middle - 3.0, 0.0)),
        jnp.minimum(at[4], jnp.ceil(middle) + 3.0),
    )
    m4 = at[4] - p4
    plus = [None] * 5
    minus = [None] * 5
    plus[4], minus[4] = p4, m4
    for j in (3, 2, 1):
        plus[j] = plus[j + 1] + at[j]
        minus[j] = minus[j + 1] + at[8 - j]
    nil = jnp.zeros_like(p4)
    offset = [nil, plus[2], plus[3], plus[4], nil, minus[4], minus[3], minus[2]]

    needs = [(jnp.maximum(jnp.max(plus[j]), jnp.max(minus[j])), j - 1) for j in (1, 2, 3, 4)]
    level = jnp.int32(0)
    for caps in LEVELS[:-1]:
        over = jnp.int32(0)
        for need, j in needs:
            over = jnp.maximum(over, jnp.where(need > float(caps[j]), 1, 0))
        level = level + over
    level_ref[0] = level

    def column(row, e):
        return jnp.sum(jnp.where(lax.broadcasted_iota(I32, (1, 128), 1) == e, row, 0.0), axis=1, keepdims=True)

    mine = src == me
    rank = ranks(jnp.where(mine, 1.0, 0.0))
    away = (slot // 8 - z) & 7
    half = column(p4, me)
    place = rank
    for k in range(1, 8):
        base = OWN if k < 4 else OWN + SEND_MINUS
        value = column(offset[k], me) + rank + float(base)
        if k == 4:
            value = jnp.where(rank < half, rank + float(OWN), rank - half + float(OWN + SEND_MINUS))
        place = jnp.where(away == k, value, place)
    place = jnp.where(mine, place, -1.0)

    def first_list(g, _):
        rows = []
        for i in range(8):
            k = (g * 8 + i).astype(F32)
            rows.append(jnp.sum(jnp.where(place == k, loc, 0.0), axis=0, keepdims=True))
        list_s[pl.ds(pl.multiple_of(g * 8, 8), 8), :] = jnp.concatenate(rows, axis=0)
        return 0

    lax.fori_loop(0, LIST // 8, first_list, 0)
    ones = jnp.ones((8, 128), F32)
    t12_ref[0:8, :] = dot(ones, list_s[...], ((1,), (1,)), lax.Precision.HIGHEST).astype(I32)

    row8 = pl.ds(pl.multiple_of(z * 8, 8), 8)
    src_r = src_s[row8, :]
    marks = jnp.concatenate([jnp.where(src_r == zs * NX + x, 1.0, 0.0) for zs in range(NZ)], axis=0)
    rank = ranks(marks)
    off8 = jnp.concatenate(offset, axis=0)
    k8 = lax.broadcasted_iota(I32, (8, 128), 0)
    e8 = lax.broadcasted_iota(I32, (8, 128), 1)
    here = (e8 & 3) == x
    off_e = jnp.sum(jnp.where(here & (k8 == ((z - e8 // NX) & 7)), off8, 0.0), axis=0, keepdims=True)
    half_e = jnp.where(here[0:1], p4, 0.0)
    through = jnp.zeros((8, 128), F32)
    for zs in range(NZ):
        r = rank[zs * 8 : zs * 8 + 8]
        pick = (e8[0:1] // NX) == zs
        off = jnp.sum(jnp.where(pick, off_e, 0.0), axis=1, keepdims=True)
        half = jnp.sum(jnp.where(pick, half_e, 0.0), axis=1, keepdims=True)
        d = jnp.broadcast_to((z - zs) & 7, (8, 128))
        value = r
        for k in range(1, 8):
            if k == 4:
                v = jnp.where(r < half, r + float(PLUS[3]), r - half + float(MINUS[3]))
            else:
                v = off + r + float(PLUS[k - 1] if k < 4 else MINUS[7 - k])
            value = jnp.where(d == k, v, value)
        through = through + marks[zs * 8 : zs * 8 + 8] * value

    used_r = src_r < 32
    odd = (k8 & 1) == 1
    apart = (z - (src_r >> 2)) & 7
    far = (apart >= 3) & (apart <= 5)
    order = jnp.where(far, float(XNEAR), 0.0)
    for k in range(2 * NX):
        mark = jnp.where(used_r & ((src_r & 3) == k // 2) & (far if k % 2 else ~far), 1.0, 0.0)
        total = jnp.broadcast_to(jnp.sum(mark, axis=1, keepdims=True), (8, 128))
        r = dot(mark.astype(BF), tri, ((1,), (0,))) + jnp.where(odd, pltpu.roll(total, 1, 0), 0.0)
        order = order + mark * r
    order_i = order.astype(I32)
    t3_ref[...] = jnp.where(used_r, ((src_r - x) & 3) * XFULL + order_i, 0)
    lens_ref[...] = longs[row8, :]
    goes = ((k8 // 2 - x) & 3) * XFULL + order_i
    goes = jnp.where(used_r & ((src_r & 3) == x), goes, -1)

    def second_list(g, _):
        rows = []
        for i in range(8):
            rows.append(jnp.sum(jnp.where(goes == g * 8 + i, through, 0.0), axis=0, keepdims=True))
        list_s[pl.ds(pl.multiple_of(g * 8, 8), 8), :] = jnp.concatenate(rows, axis=0)
        return 0

    lax.fori_loop(0, LIST // 8, second_list, 0)
    t12_ref[8:16, :] = dot(ones, list_s[...], ((1,), (1,)), lax.Precision.HIGHEST).astype(I32)


def make_tables(mem_len, assign, block_table):
    smem = pl.BlockSpec(memory_space=pltpu.SMEM)
    vmem = pl.BlockSpec(memory_space=pltpu.VMEM)
    return pl.pallas_call(
        tables_kernel,
        out_shape=(
            jax.ShapeDtypeStruct((8, 128), I32),
            jax.ShapeDtypeStruct((16, LIST), I32),
            jax.ShapeDtypeStruct((8, 128), I32),
            jax.ShapeDtypeStruct((1,), I32),
        ),
        in_specs=[smem, smem, vmem],
        out_specs=(vmem, vmem, vmem, smem),
        scratch_shapes=[
            pltpu.VMEM((64, 128), I32),
            pltpu.VMEM((64, 128), I32),
            pltpu.VMEM((64, 128), I32),
            pltpu.VMEM((64, 128), I32),
            pltpu.VMEM((LIST, 128), F32),
        ],
    )(mem_len, assign, block_table)


def handoff_kernel(caps, *refs):
    n = len(CHUNKS)
    it = iter(refs)
    t3, t12, lens, q_ref, nk_ref, nv_ref, kp_hbm, vp_hbm, w_hbm = (next(it) for _ in range(9))
    lo_ref, ko_hbm, vo_hbm = (next(it) for _ in range(3))
    pools = (next(it), next(it))
    staged = (next(it), next(it))
    zs = [next(it) for _ in range(n)]
    zb = [(next(it), next(it)) for _ in range(n)]
    xs = [next(it) for _ in range(n)]
    xb = [next(it) for _ in range(n)]
    probs, att, wbuf, abuf, part, rbuf, fin_s, fin = (next(it) for _ in range(8))
    local_sem, z_send, z_recv, x_send, x_recv, w_send, w_recv, a_send, a_recv, r_send, r_recv, f_send, f_recv = it

    me, tp = lax.axis_index("dp"), lax.axis_index("tp")
    z, x = me // NX, me % NX
    z_to = [{"dp": ((z + 1) % NZ) * NX + x}, {"dp": ((z + NZ - 1) % NZ) * NX + x}]
    x_to = [{"dp": z * NX + (x + r) % NX} for r in range(NX)]
    t_to = [{"tp": (tp + r) % NT} for r in range(NT)]

    loads = [
        pltpu.make_async_copy(kp_hbm, pools[0], local_sem.at[0]),
        pltpu.make_async_copy(vp_hbm, pools[1], local_sem.at[1]),
        pltpu.make_async_copy(w_hbm, wbuf.at[0], local_sem.at[2]),
    ]
    for c in loads:
        c.start()
    barrier = pltpu.get_barrier_semaphore()
    peers = z_to + x_to[1:] + t_to[1:]
    for d in peers:
        pl.semaphore_signal(barrier, inc=1, device_id=d, device_id_type=MESH)

    def remote(src, dst, ss, rs, to):
        return pltpu.make_async_remote_copy(
            src_ref=src, dst_ref=dst, send_sem=ss, recv_sem=rs, device_id=to, device_id_type=MESH
        )

    sent = []

    def z_copy(c, d, j):
        base = (PLUS, MINUS)[d]
        if j == 1:
            src = zs[c].at[pl.ds(d * SEND_MINUS, caps[0])]
        else:
            src = zb[c][(j - 2) // 2].at[pl.ds(base[j - 2], caps[j - 1])]
        dst = zb[c][(j - 1) // 2].at[pl.ds(base[j - 1], caps[j - 1])]
        return remote(src, dst, z_send.at[c, d, j - 1], z_recv.at[c, d, j - 1], z_to[d])

    def z_start(c, j):
        for d in range(2):
            cp = z_copy(c, d, j)
            cp.start()
            sent.append(cp)

    spans = ((0, XNEAR), (XNEAR, XFULL - XNEAR))

    def x_copy(c, r, far):
        first, pages = spans[far]
        return remote(
            xs[c].at[pl.ds((r - 1) * XFULL + first, pages)],
            xb[c].at[pl.ds((NX - r) * XFULL + first, pages)],
            x_send.at[c, far, r - 1],
            x_recv.at[c, far, r - 1],
            x_to[r],
        )

    def pack_pool(which):
        mine = [(c, r0, rows) for c, (w, r0, rows) in enumerate(CHUNKS) if w == which]
        pool = pools[which]

        def body(first, dst, place, k, _):
            got = pool[t12[0, first + k]]
            for c, r0, rows in mine:
                dst[c][place + k] = got[r0 : r0 + rows]
            return 0

        near = [z[0] for z in zb]

        lax.fori_loop(0, OWN, functools.partial(body, 0, near, 0), 0, unroll=4)
        lax.fori_loop(0, caps[0], functools.partial(body, OWN, zs, 0), 0, unroll=2)
        lax.fori_loop(0, caps[0], functools.partial(body, OWN + SEND_MINUS, zs, SEND_MINUS), 0, unroll=2)

    def pack_row(c, far):
        start, pages = spans[far]

        def body(first, dst, place, k, _):
            dst[place + k] = zb[c][far][t12[8, first + k]]
            return 0

        for r in (2, 1, 3):
            put = functools.partial(body, r * XFULL + start, xs[c], (r - 1) * XFULL + start)
            lax.fori_loop(0, pages, put, 0, unroll=5)
            cp = x_copy(c, r, far)
            cp.start()
            sent.append(cp)
        lax.fori_loop(0, pages, functools.partial(body, start, xb[c], start), 0, unroll=5)

    def place_pages(c):
        which, r0, rows = CHUNKS[c]
        token = lax.broadcasted_iota(I32, (rows, HD), 0)
        for s in range(2):

            def body(p, _):
                got = xb[c][t3[2 * x + s, p]]
                left = lens[2 * x + s, 0] - p * PAGE - r0
                got = jnp.where(token < left, got.astype(F32), 0.0).astype(BF)
                staged[which][s, pl.ds(pl.multiple_of(p * PAGE + r0, 16), rows), :] = got
                return 0

            lax.fori_loop(0, PAGES, body, 0, unroll=4)

    scale = 1.0 / math.sqrt(HD)
    tile = 512

    def queries_of(s):
        rows = q_ref[s * 32 : (s + 1) * 32, :]
        return jnp.concatenate([rows[:, h * HD : (h + 1) * HD] for h in range(QPK)], axis=0)

    def fresh_scores(s):
        sc = dot(queries_of(s), nk_ref[s * 32 : (s + 1) * 32, :], ((1,), (1,))) * scale
        r = lax.broadcasted_iota(I32, sc.shape, 0) % 32
        u = lax.broadcasted_iota(I32, sc.shape, 1)
        ok = (r // 4 == u // 4) & (u % 4 <= r % 4)
        return jnp.where(ok, sc, -jnp.inf)

    def tile_scores(s, q, i, length):
        keys = staged[0][s, pl.ds(pl.multiple_of(i * tile, tile), tile), :]
        sc = dot(q, keys, ((1,), (1,))) * scale
        pos = lax.broadcasted_iota(I32, sc.shape, 1) + i * tile
        return jnp.where(pos < length, sc, -jnp.inf)

    def find_max(s):
        q = queries_of(s)
        length = lens[2 * x + s, 0]

        def body(i, m):
            sc = tile_scores(s, q, i, length)
            for k in range(tile // 128):
                m = jnp.maximum(m, sc[:, k * 128 : (k + 1) * 128])
            return m

        m = lax.fori_loop(0, SPAN // tile, body, jnp.full((256, 128), -jnp.inf, F32))
        top = jnp.maximum(jnp.max(m, axis=1, keepdims=True), jnp.max(fresh_scores(s), axis=1, keepdims=True))
        att[s, 0] = jnp.broadcast_to(top, (256, 128))

    def weigh(s):
        q = queries_of(s)
        length = lens[2 * x + s, 0]
        top = att[s, 0][:, 0:1]

        def body(i, t):
            w = jnp.exp(tile_scores(s, q, i, length) - top)
            probs[s, :, pl.ds(pl.multiple_of(i * tile, tile), tile)] = w.astype(BF)
            for k in range(tile // 128):
                t = t + w[:, k * 128 : (k + 1) * 128]
            return t

        t = lax.fori_loop(0, SPAN // tile, body, jnp.zeros((256, 128), F32))
        fresh = jnp.exp(fresh_scores(s) - top)
        total = jnp.sum(t, axis=1, keepdims=True) + jnp.sum(fresh, axis=1, keepdims=True)
        att[s, 0] = jnp.broadcast_to(total, (256, 128))
        att[s, 1] = dot(fresh.astype(BF), nv_ref[s * 32 : (s + 1) * 32, :], ((1,), (0,)))

    def finish(s):
        acc = att[s, 1]

        def body(i, a):
            at = pl.ds(pl.multiple_of(i * 1024, 1024), 1024)
            return a + dot(probs[s, :, at], staged[1][s, at, :], ((1,), (0,)))

        acc = lax.fori_loop(0, SPAN // 1024, body, acc)
        rows = (acc / att[s, 0]).astype(BF)
        for h in range(QPK):
            abuf[0, s * 32 : (s + 1) * 32, h * HD : (h + 1) * HD] = rows[h * 32 : (h + 1) * 32, :]

    half = wbuf.shape[1] // 2

    def w_copy(i):
        src, dst, r = (
            (wbuf.at[0], wbuf.at[3], 1),
            (wbuf.at[0], wbuf.at[1], 3),
            (wbuf.at[3, pl.ds(0, half)], wbuf.at[2, pl.ds(0, half)], 1),
            (wbuf.at[1, pl.ds(half, half)], wbuf.at[2, pl.ds(half, half)], 3),
        )[i]
        return remote(src, dst, w_send.at[i], w_recv.at[i], x_to[r])

    def w_start(i):
        cp = w_copy(i)
        cp.start()
        sent.append(cp)

    pl.semaphore_wait(barrier, len(peers))
    loads[0].wait()
    pack_pool(0)
    z_start(0, 1)
    z_start(1, 1)
    loads[2].wait()
    w_start(0)
    w_start(1)
    loads[1].wait()
    pack_pool(1)

    k_last = max(c for c, ch in enumerate(CHUNKS) if ch[0] == 0)
    work = [functools.partial(f, s) for f in (find_max, weigh) for s in range(2)]
    flush = []
    for r in range(1, n + 5):
        for c in range(max(0, r - 4), min(n, r)):
            j = r - c
            for d in range(2):
                z_copy(c, d, j).wait_recv()
            if j < 4:
                z_start(c, j + 1)
        if r + 1 < n:
            z_start(r + 1, 1)
        if r == 2:
            w_copy(0).wait_recv()
            w_copy(1).wait_recv()
            w_start(2)
            w_start(3)
        if 0 <= r - 4 < n:
            pack_row(r - 4, 1)
        if 0 <= r - 2 < n:
            pack_row(r - 2, 0)
        if 0 <= r - 5 < n:
            c = r - 5
            for far in range(2):
                for i in (1, 2, 3):
                    x_copy(c, i, far).wait_recv()
            place_pages(c)
            if c == k_last:
                out = pltpu.make_async_copy(staged[0], ko_hbm, local_sem.at[3])
                out.start()
                flush.append(out)
        for _ in range({8: 2, 9: 1, 11: 1}.get(r, 0)):
            work.pop(0)()
    out = pltpu.make_async_copy(staged[1], vo_hbm, local_sem.at[4])
    out.start()
    flush.append(out)

    def a_copy(s, d, j):
        rows = pl.ds(s * 32, 32)
        here = (j - 1) if d == 0 else (9 - j) % 8
        there = j if d == 0 else 8 - j
        return remote(abuf.at[here, rows], abuf.at[there, rows], a_send.at[s, d, j - 1], a_recv.at[s, d, j - 1], z_to[d])

    def a_start(s, d, j):
        cp = a_copy(s, d, j)
        cp.start()
        sent.append(cp)

    for s in range(2):
        finish(s)
        for d in range(2):
            a_start(s, d, 1)

    w_copy(2).wait_recv()
    w_copy(3).wait_recv()

    def block_copy(r):
        return remote(part.at[r], rbuf.at[tp], r_send.at[r], r_recv.at[tp], {"tp": (z + NZ - r) % NZ})

    def project(r):
        rows = abuf[r]
        for k in range(NX):
            part[r, :, k * 256 : (k + 1) * 256] = dot(rows, wbuf[k], ((1,), (0,))).astype(BF)
        target = (z + NZ - r) % NZ

        @pl.when(target != tp)
        def _():
            block_copy(r).start()

        @pl.when(target == tp)
        def _():
            rbuf[tp] = part[r]

    project(0)
    for j in (1, 2, 3, 4):
        for s in range(2):
            for d in range(2):
                if j < 4 or s == d:
                    a_copy(s, d, j).wait_recv()
                if j < 3 or (j == 3 and s == d):
                    a_start(s, d, j + 1)
        project(j)
        if j < 4:
            project(8 - j)

    total = jnp.zeros((64, 1024), F32)
    for t in range(NT):

        @pl.when(t != tp)
        def _():
            remote(part.at[0], rbuf.at[t], r_send.at[0], r_recv.at[t], t_to[1]).wait_recv()

    for t in range(NT):
        total = total + rbuf[t].astype(F32)
    total = total.astype(BF)
    rows = pl.ds(pl.multiple_of(x * 64, 64), 64)
    fin[rows, :] = total[:, 0:256]
    for k in range(1, NX):
        fin_s[k - 1] = total[:, k * 256 : (k + 1) * 256]
        cp = remote(fin_s.at[k - 1], fin.at[rows], f_send.at[k - 1], f_recv.at[k - 1], x_to[k])
        cp.start()
        sent.append(cp)
    for k in range(1, NX):
        from_rows = pl.ds(pl.multiple_of(((x + NX - k) % NX) * 64, 64), 64)
        remote(fin_s.at[k - 1], fin.at[from_rows], f_send.at[k - 1], f_recv.at[k - 1], x_to[k]).wait_recv()
    lo_ref[...] = fin[...]
    for r in range(NZ):

        @pl.when((z + NZ - r) % NZ != tp)
        def _():
            block_copy(r).wait_send()

    for cp in sent:
        cp.wait_send()
    for cp in flush:
        cp.wait()


def handoff(level, t3, t12, lens, q, nk, nv, key_pool, value_pool, out_weight):
    caps = LEVELS[level]
    n = len(CHUNKS)
    smem = pl.BlockSpec(memory_space=pltpu.SMEM)
    vmem = pl.BlockSpec(memory_space=pltpu.VMEM)
    hbm = pl.BlockSpec(memory_space=pl.ANY)
    dma = pltpu.SemaphoreType.DMA
    scratch = [pltpu.VMEM((POOL, PAGE, HD), BF)] * 2 + [pltpu.VMEM((2, SPAN, HD), BF)] * 2
    for pages in ((2 * SEND_MINUS,), ZROOM, (3 * XFULL,), (4 * XFULL,)):
        scratch += [pltpu.VMEM((k, rows, HD), BF) for _, _, rows in CHUNKS for k in pages]
    scratch += [
        pltpu.VMEM((2, 256, SPAN), BF),
        pltpu.VMEM((2, 2, 256, 128), F32),
        pltpu.VMEM((NX, 1024, 256), BF),
        pltpu.VMEM((NZ, 64, 1024), BF),
        pltpu.VMEM((NZ, 64, 1024), BF),
        pltpu.VMEM((NT, 64, 1024), BF),
        pltpu.VMEM((3, 64, 256), BF),
        pltpu.VMEM((256, 256), BF),
        dma((5,)),
        dma((n, 2, 4)),
        dma((n, 2, 4)),
        dma((n, 2, 3)),
        dma((n, 2, 3)),
        dma((4,)),
        dma((4,)),
        dma((2, 2, 4)),
        dma((2, 2, 4)),
        dma((NZ,)),
        dma((NT,)),
        dma((3,)),
        dma((3,)),
    ]
    return pl.pallas_call(
        functools.partial(handoff_kernel, caps),
        out_shape=(
            jax.ShapeDtypeStruct((256, 256), BF),
            jax.ShapeDtypeStruct((2, SPAN, HD), BF),
            jax.ShapeDtypeStruct((2, SPAN, HD), BF),
        ),
        in_specs=[smem] * 3 + [vmem] * 3 + [hbm] * 3,
        out_specs=(vmem, hbm, hbm),
        scratch_shapes=scratch,
        compiler_params=pltpu.CompilerParams(
            collective_id=level, has_side_effects=True, vmem_limit_bytes=58 * 2**20
        ),
    )(t3, t12, lens, q, nk, nv, key_pool, value_pool, out_weight)


def local(queries, new_keys, new_values, key_pool, value_pool, out_weight, mem_len, assign, block_table):
    t3, t12, lens, level = make_tables(mem_len, assign, block_table)
    q = queries.reshape(64, 1024)
    nk = new_keys.reshape(64, HD)
    nv = new_values.reshape(64, HD)
    branches = [functools.partial(handoff, i) for i in range(len(LEVELS))]
    return lax.switch(level[0], branches, t3, t12, lens, q, nk, nv, key_pool, value_pool, out_weight)


def solution(mesh):
    placed = (
        P("dp", None, None, "tp"),
        P("dp", None, None, "tp"),
        P("dp", None, None, "tp"),
        P("dp", None, "tp"),
        P("dp", None, "tp"),
        P("tp", "dp"),
        P(),
        P(),
        P(),
    )
    return jax.shard_map(
        local,
        mesh=mesh,
        in_specs=placed,
        out_specs=(P("tp", "dp"), P("dp", None, "tp"), P("dp", None, "tp")),
        check_vma=False,
    )
```

```python
import functools
import math

import jax
import jax.numpy as jnp
from jax import lax
from jax.experimental import pallas as pl
from jax.experimental.pallas import tpu as pltpu
from jax.sharding import PartitionSpec as P

MESH = pl.DeviceIdType.MESH
BF = jnp.bfloat16
F32 = jnp.float32
I32 = jnp.int32

NZ, NX, NT = 8, 4, 8
HD = 128
QPK = 8
PAGE = 64
PAGES = 80
POOL = 160
SPAN = PAGES * PAGE

FULL = (73, 53, 33, 13)
XFULL = 40
LEVELS = (
    (36, 28, 19, 9),
    (39, 30, 21, 10),
    (45, 34, 24, 12),
    FULL,
)
OWN = 20
PLUS = (20, 93, 0, 33)
MINUS = (146, 219, 46, 79)
ZROOM = (272, 92)
XNEAR = 25
SEND_MINUS = FULL[0]
LIST = 168
CHUNKS = tuple((w, r, 16) for w in (0, 1) for r in (0, 16, 32, 48))


def dot(a, b, dims, precision=None):
    return lax.dot_general(a, b, (dims, ((), ())), precision=precision, preferred_element_type=F32)


def tables_kernel(len_ref, assign_ref, bt_ref, t3_ref, t12_ref, lens_ref, level_ref, raw, longs, src_s, used_s, list_s):
    me = lax.axis_index("dp")
    z, x = me // NX, me % NX
    raw[...] = jnp.zeros_like(raw)
    for s in range(64):
        a = assign_ref[s]
        raw[s : s + 1, 0:PAGES] = bt_ref[pl.ds(a, 1), :]
        longs[s : s + 1, :] = jnp.full((1, 128), len_ref[a], I32)

    shape = (64, 128)
    slot = lax.broadcasted_iota(I32, shape, 0)
    lane = lax.broadcasted_iota(I32, shape, 1)
    page = raw[...]
    src = (page * 26215) >> 22
    loc = (page - src * POOL).astype(F32)
    used = jnp.where((lane < PAGES) & (lane * PAGE < longs[...]), 1, 0)
    src = jnp.where(used == 1, src, 1000)
    src_s[...] = src

    tri = jnp.where(lax.broadcasted_iota(I32, (128, 128), 0) < lax.broadcasted_iota(I32, (128, 128), 1), 1.0, 0.0).astype(BF)
    bi, bj = lax.broadcasted_iota(I32, (64, 64), 0), lax.broadcasted_iota(I32, (64, 64), 1)
    blocks = jnp.where((bi // 8 == bj // 8) & (bj < bi), 1.0, 0.0).astype(BF)

    def ranks(mask):
        total = jnp.broadcast_to(jnp.sum(mask, axis=1, keepdims=True), shape)
        return dot(mask.astype(BF), tri, ((1,), (0,))) + dot(blocks, total.astype(BF), ((1,), (0,)))

    count = jnp.zeros(shape, F32)
    for e in range(32):
        total = jnp.sum(jnp.where(src == e, 1.0, 0.0), axis=1, keepdims=True)
        count = jnp.where(lane == e, total, count)
    dist = (slot // 8 - lane // NX) & 7
    at = [jnp.sum(jnp.where((dist == k) & (lane < 32), count, 0.0), axis=0, keepdims=True) for k in range(8)]
    lean = (at[5] + at[6] + at[7] - at[1] - at[2] - at[3]) * 0.25
    middle = at[4] * 0.5
    p4 = jnp.clip(
        jnp.floor(middle + lean + 0.5),
        jnp.floor(jnp.maximum(middle - 3.0, 0.0)),
        jnp.minimum(at[4], jnp.ceil(middle) + 3.0),
    )
    m4 = at[4] - p4
    plus = [None] * 5
    minus = [None] * 5
    plus[4], minus[4] = p4, m4
    for j in (3, 2, 1):
        plus[j] = plus[j + 1] + at[j]
        minus[j] = minus[j + 1] + at[8 - j]
    nil = jnp.zeros_like(p4)
    offset = [nil, plus[2], plus[3], plus[4], nil, minus[4], minus[3], minus[2]]

    needs = [(jnp.maximum(jnp.max(plus[j]), jnp.max(minus[j])), j - 1) for j in (1, 2, 3, 4)]
    level = jnp.int32(0)
    for caps in LEVELS[:-1]:
        over = jnp.int32(0)
        for need, j in needs:
            over = jnp.maximum(over, jnp.where(need > float(caps[j]), 1, 0))
        level = level + over
    level_ref[0] = level

    def column(row, e):
        return jnp.sum(jnp.where(lax.broadcasted_iota(I32, (1, 128), 1) == e, row, 0.0), axis=1, keepdims=True)

    mine = src == me
    rank = ranks(jnp.where(mine, 1.0, 0.0))
    away = (slot // 8 - z) & 7
    half = column(p4, me)
    place = rank
    for k in range(1, 8):
        base = OWN if k < 4 else OWN + SEND_MINUS
        value = column(offset[k], me) + rank + float(base)
        if k == 4:
            value = jnp.where(rank < half, rank + float(OWN), rank - half + float(OWN + SEND_MINUS))
        place = jnp.where(away == k, value, place)
    place = jnp.where(mine, place, -1.0)

    def first_list(g, _):
        rows = []
        for i in range(8):
            k = (g * 8 + i).astype(F32)
            rows.append(jnp.sum(jnp.where(place == k, loc, 0.0), axis=0, keepdims=True))
        list_s[pl.ds(pl.multiple_of(g * 8, 8), 8), :] = jnp.concatenate(rows, axis=0)
        return 0

    lax.fori_loop(0, LIST // 8, first_list, 0)
    ones = jnp.ones((8, 128), F32)
    t12_ref[0:8, :] = dot(ones, list_s[...], ((1,), (1,)), lax.Precision.HIGHEST).astype(I32)

    row8 = pl.ds(pl.multiple_of(z * 8, 8), 8)
    src_r = src_s[row8, :]
    marks = jnp.concatenate([jnp.where(src_r == zs * NX + x, 1.0, 0.0) for zs in range(NZ)], axis=0)
    rank = ranks(marks)
    off8 = jnp.concatenate(offset, axis=0)
    k8 = lax.broadcasted_iota(I32, (8, 128), 0)
    e8 = lax.broadcasted_iota(I32, (8, 128), 1)
    here = (e8 & 3) == x
    off_e = jnp.sum(jnp.where(here & (k8 == ((z - e8 // NX) & 7)), off8, 0.0), axis=0, keepdims=True)
    half_e = jnp.where(here[0:1], p4, 0.0)
    through = jnp.zeros((8, 128), F32)
    for zs in range(NZ):
        r = rank[zs * 8 : zs * 8 + 8]
        pick = (e8[0:1] // NX) == zs
        off = jnp.sum(jnp.where(pick, off_e, 0.0), axis=1, keepdims=True)
        half = jnp.sum(jnp.where(pick, half_e, 0.0), axis=1, keepdims=True)
        d = jnp.broadcast_to((z - zs) & 7, (8, 128))
        value = r
        for k in range(1, 8):
            if k == 4:
                v = jnp.where(r < half, r + float(PLUS[3]), r - half + float(MINUS[3]))
            else:
                v = off + r + float(PLUS[k - 1] if k < 4 else MINUS[7 - k])
            value = jnp.where(d == k, v, value)
        through = through + marks[zs * 8 : zs * 8 + 8] * value

    used_r = src_r < 32
    odd = (k8 & 1) == 1
    apart = (z - (src_r >> 2)) & 7
    far = (apart >= 3) & (apart <= 5)
    order = jnp.where(far, float(XNEAR), 0.0)
    for k in range(2 * NX):
        mark = jnp.where(used_r & ((src_r & 3) == k // 2) & (far if k % 2 else ~far), 1.0, 0.0)
        total = jnp.broadcast_to(jnp.sum(mark, axis=1, keepdims=True), (8, 128))
        r = dot(mark.astype(BF), tri, ((1,), (0,))) + jnp.where(odd, pltpu.roll(total, 1, 0), 0.0)
        order = order + mark * r
    order_i = order.astype(I32)
    t3_ref[...] = jnp.where(used_r, ((src_r - x) & 3) * XFULL + order_i, 0)
    lens_ref[...] = longs[row8, :]
    goes = ((k8 // 2 - x) & 3) * XFULL + order_i
    goes = jnp.where(used_r & ((src_r & 3) == x), goes, -1)

    def second_list(g, _):
        rows = []
        for i in range(8):
            rows.append(jnp.sum(jnp.where(goes == g * 8 + i, through, 0.0), axis=0, keepdims=True))
        list_s[pl.ds(pl.multiple_of(g * 8, 8), 8), :] = jnp.concatenate(rows, axis=0)
        return 0

    lax.fori_loop(0, LIST // 8, second_list, 0)
    t12_ref[8:16, :] = dot(ones, list_s[...], ((1,), (1,)), lax.Precision.HIGHEST).astype(I32)


def make_tables(mem_len, assign, block_table):
    smem = pl.BlockSpec(memory_space=pltpu.SMEM)
    vmem = pl.BlockSpec(memory_space=pltpu.VMEM)
    return pl.pallas_call(
        tables_kernel,
        out_shape=(
            jax.ShapeDtypeStruct((8, 128), I32),
            jax.ShapeDtypeStruct((16, LIST), I32),
            jax.ShapeDtypeStruct((8, 128), I32),
            jax.ShapeDtypeStruct((1,), I32),
        ),
        in_specs=[smem, smem, vmem],
        out_specs=(vmem, vmem, vmem, smem),
        scratch_shapes=[
            pltpu.VMEM((64, 128), I32),
            pltpu.VMEM((64, 128), I32),
            pltpu.VMEM((64, 128), I32),
            pltpu.VMEM((64, 128), I32),
            pltpu.VMEM((LIST, 128), F32),
        ],
    )(mem_len, assign, block_table)


def handoff_kernel(caps, *refs):
    n = len(CHUNKS)
    it = iter(refs)
    t3, t12, lens, q_ref, nk_ref, nv_ref, kp_hbm, vp_hbm, w_hbm = (next(it) for _ in range(9))
    lo_ref, ko_hbm, vo_hbm = (next(it) for _ in range(3))
    pools = (next(it), next(it))
    staged = (next(it), next(it))
    zs = [next(it) for _ in range(n)]
    zb = [(next(it), next(it)) for _ in range(n)]
    xs = [next(it) for _ in range(n)]
    xb = [next(it) for _ in range(n)]
    probs, att, wbuf, abuf, part, rbuf, fin_s, fin = (next(it) for _ in range(8))
    local_sem, z_send, z_recv, x_send, x_recv, w_send, w_recv, a_send, a_recv, r_send, r_recv, f_send, f_recv = it

    me, tp = lax.axis_index("dp"), lax.axis_index("tp")
    z, x = me // NX, me % NX
    z_to = [{"dp": ((z + 1) % NZ) * NX + x}, {"dp": ((z + NZ - 1) % NZ) * NX + x}]
    x_to = [{"dp": z * NX + (x + r) % NX} for r in range(NX)]
    t_to = [{"tp": (tp + r) % NT} for r in range(NT)]

    loads = [
        pltpu.make_async_copy(kp_hbm, pools[0], local_sem.at[0]),
        pltpu.make_async_copy(vp_hbm, pools[1], local_sem.at[1]),
        pltpu.make_async_copy(w_hbm, wbuf.at[0], local_sem.at[2]),
    ]
    for c in loads:
        c.start()
    barrier = pltpu.get_barrier_semaphore()
    peers = z_to + x_to[1:] + t_to[1:]
    for d in peers:
        pl.semaphore_signal(barrier, inc=1, device_id=d, device_id_type=MESH)

    def remote(src, dst, ss, rs, to):
        return pltpu.make_async_remote_copy(
            src_ref=src, dst_ref=dst, send_sem=ss, recv_sem=rs, device_id=to, device_id_type=MESH
        )

    sent = []

    def z_copy(c, d, j):
        base = (PLUS, MINUS)[d]
        if j == 1:
            src = zs[c].at[pl.ds(d * SEND_MINUS, caps[0])]
        else:
            src = zb[c][(j - 2) // 2].at[pl.ds(base[j - 2], caps[j - 1])]
        dst = zb[c][(j - 1) // 2].at[pl.ds(base[j - 1], caps[j - 1])]
        return remote(src, dst, z_send.at[c, d, j - 1], z_recv.at[c, d, j - 1], z_to[d])

    def z_start(c, j):
        for d in range(2):
            cp = z_copy(c, d, j)
            cp.start()
            sent.append(cp)

    spans = ((0, XNEAR), (XNEAR, XFULL - XNEAR))

    def x_copy(c, r, far):
        first, pages = spans[far]
        return remote(
            xs[c].at[pl.ds((r - 1) * XFULL + first, pages)],
            xb[c].at[pl.ds((NX - r) * XFULL + first, pages)],
            x_send.at[c, far, r - 1],
            x_recv.at[c, far, r - 1],
            x_to[r],
        )

    def pack_pool(which):
        mine = [(c, r0, rows) for c, (w, r0, rows) in enumerate(CHUNKS) if w == which]
        pool = pools[which]

        def body(first, dst, place, k, _):
            got = pool[t12[0, first + k]]
            for c, r0, rows in mine:
                dst[c][place + k] = got[r0 : r0 + rows]
            return 0

        near = [z[0] for z in zb]

        lax.fori_loop(0, OWN, functools.partial(body, 0, near, 0), 0, unroll=4)
        lax.fori_loop(0, caps[0], functools.partial(body, OWN, zs, 0), 0, unroll=2)
        lax.fori_loop(0, caps[0], functools.partial(body, OWN + SEND_MINUS, zs, SEND_MINUS), 0, unroll=2)

    def pack_row(c, far):
        start, pages = spans[far]

        def body(first, dst, place, k, _):
            dst[place + k] = zb[c][far][t12[8, first + k]]
            return 0

        for r in (2, 1, 3):
            put = functools.partial(body, r * XFULL + start, xs[c], (r - 1) * XFULL + start)
            lax.fori_loop(0, pages, put, 0, unroll=5)
            cp = x_copy(c, r, far)
            cp.start()
            sent.append(cp)
        lax.fori_loop(0, pages, functools.partial(body, start, xb[c], start), 0, unroll=5)

    def place_pages(c):
        which, r0, rows = CHUNKS[c]
        token = lax.broadcasted_iota(I32, (rows, HD), 0)
        def slot(s, _):
            length = lens[2 * x + s, 0] - r0

            def body(p, _):
                got = xb[c][t3[2 * x + s, p]]
                got = jnp.where(token < length - p * PAGE, got.astype(F32), 0.0).astype(BF)
                staged[which][s, pl.ds(pl.multiple_of(p * PAGE + r0, 16), rows), :] = got
                return 0

            return lax.fori_loop(0, PAGES, body, 0, unroll=4)

        lax.fori_loop(0, 2, slot, 0)

    scale = 1.0 / math.sqrt(HD)
    tile = 512

    def slot_rows(s):
        return pl.ds(pl.multiple_of(s * 32, 32), 32)

    def queries_of(s):
        rows = q_ref[slot_rows(s), :]
        return jnp.concatenate([rows[:, h * HD : (h + 1) * HD] for h in range(QPK)], axis=0)

    def fresh_scores(s):
        sc = dot(queries_of(s), nk_ref[slot_rows(s), :], ((1,), (1,))) * scale
        r = lax.broadcasted_iota(I32, sc.shape, 0) % 32
        u = lax.broadcasted_iota(I32, sc.shape, 1)
        ok = (r // 4 == u // 4) & (u % 4 <= r % 4)
        return jnp.where(ok, sc, -jnp.inf)

    def tile_scores(s, q, i, length):
        keys = staged[0][s, pl.ds(pl.multiple_of(i * tile, tile), tile), :]
        sc = dot(q, keys, ((1,), (1,))) * scale
        pos = lax.broadcasted_iota(I32, sc.shape, 1) + i * tile
        return jnp.where(pos < length, sc, -jnp.inf)

    def find_max(s):
        q = queries_of(s)
        length = lens[2 * x + s, 0]

        def body(i, m):
            sc = tile_scores(s, q, i, length)
            for k in range(tile // 128):
                m = jnp.maximum(m, sc[:, k * 128 : (k + 1) * 128])
            return m

        m = lax.fori_loop(0, SPAN // tile, body, jnp.full((256, 128), -jnp.inf, F32))
        top = jnp.maximum(jnp.max(m, axis=1, keepdims=True), jnp.max(fresh_scores(s), axis=1, keepdims=True))
        att[s, 0] = jnp.broadcast_to(top, (256, 128))

    def weigh(s):
        q = queries_of(s)
        length = lens[2 * x + s, 0]
        top = att[s, 0][:, 0:1]

        def body(i, t):
            w = jnp.exp(tile_scores(s, q, i, length) - top)
            probs[s, :, pl.ds(pl.multiple_of(i * tile, tile), tile)] = w.astype(BF)
            for k in range(tile // 128):
                t = t + w[:, k * 128 : (k + 1) * 128]
            return t

        t = lax.fori_loop(0, SPAN // tile, body, jnp.zeros((256, 128), F32))
        fresh = jnp.exp(fresh_scores(s) - top)
        total = jnp.sum(t, axis=1, keepdims=True) + jnp.sum(fresh, axis=1, keepdims=True)
        att[s, 0] = jnp.broadcast_to(total, (256, 128))
        att[s, 1] = dot(fresh.astype(BF), nv_ref[slot_rows(s), :], ((1,), (0,)))

    def finish(s):
        acc = att[s, 1]

        def body(i, a):
            at = pl.ds(pl.multiple_of(i * 1024, 1024), 1024)
            return a + dot(probs[s, :, at], staged[1][s, at, :], ((1,), (0,)))

        acc = lax.fori_loop(0, SPAN // 1024, body, acc)
        rows = (acc / att[s, 0]).astype(BF)
        for h in range(QPK):
            abuf[0, slot_rows(s), h * HD : (h + 1) * HD] = rows[h * 32 : (h + 1) * 32, :]

    half = wbuf.shape[1] // 2

    def w_copy(i):
        src, dst, r = (
            (wbuf.at[0], wbuf.at[3], 1),
            (wbuf.at[0], wbuf.at[1], 3),
            (wbuf.at[3, pl.ds(0, half)], wbuf.at[2, pl.ds(0, half)], 1),
            (wbuf.at[1, pl.ds(half, half)], wbuf.at[2, pl.ds(half, half)], 3),
        )[i]
        return remote(src, dst, w_send.at[i], w_recv.at[i], x_to[r])

    def w_start(i):
        cp = w_copy(i)
        cp.start()
        sent.append(cp)

    pl.semaphore_wait(barrier, len(peers))
    loads[0].wait()
    pack_pool(0)
    z_start(0, 1)
    z_start(1, 1)
    loads[2].wait()
    w_start(0)
    w_start(1)
    loads[1].wait()
    pack_pool(1)

    k_last = max(c for c, ch in enumerate(CHUNKS) if ch[0] == 0)
    def both(f):
        def body(s, _):
            f(s)
            return 0

        lax.fori_loop(0, 2, body, 0)

    flush = []
    for r in range(1, n + 5):
        for c in range(max(0, r - 4), min(n, r)):
            j = r - c
            for d in range(2):
                z_copy(c, d, j).wait_recv()
            if j < 4:
                z_start(c, j + 1)
        if r + 1 < n:
            z_start(r + 1, 1)
        if r == 2:
            w_copy(0).wait_recv()
            w_copy(1).wait_recv()
            w_start(2)
            w_start(3)
        if 0 <= r - 4 < n:
            pack_row(r - 4, 1)
        if 0 <= r - 2 < n:
            pack_row(r - 2, 0)
        if 0 <= r - 5 < n:
            c = r - 5
            for far in range(2):
                for i in (1, 2, 3):
                    x_copy(c, i, far).wait_recv()
            place_pages(c)
            if c == k_last:
                out = pltpu.make_async_copy(staged[0], ko_hbm, local_sem.at[3])
                out.start()
                flush.append(out)
        if r == n:
            both(find_max)
        if r == n + 1:
            weigh(0)
        if r == n + 3:
            weigh(1)
    out = pltpu.make_async_copy(staged[1], vo_hbm, local_sem.at[4])
    out.start()
    flush.append(out)

    def a_copy(s, d, j):
        rows = pl.ds(s * 32, 32)
        here = (j - 1) if d == 0 else (9 - j) % 8
        there = j if d == 0 else 8 - j
        return remote(abuf.at[here, rows], abuf.at[there, rows], a_send.at[s, d, j - 1], a_recv.at[s, d, j - 1], z_to[d])

    def a_start(s, d, j):
        cp = a_copy(s, d, j)
        cp.start()
        sent.append(cp)

    for s in range(2):
        finish(s)
        for d in range(2):
            a_start(s, d, 1)

    w_copy(2).wait_recv()
    w_copy(3).wait_recv()

    def block_copy(r):
        return remote(part.at[r], rbuf.at[tp], r_send.at[r], r_recv.at[tp], {"tp": (z + NZ - r) % NZ})

    def project(*blocks):
        rows = jnp.concatenate([abuf[r] for r in blocks], axis=0) if len(blocks) > 1 else abuf[blocks[0]]

        def block(k, _):
            columns = pl.ds(pl.multiple_of(k * 256, 256), 256)
            got = dot(rows, wbuf[k], ((1,), (0,))).astype(BF)
            for i, r in enumerate(blocks):
                part[r, :, columns] = got[i * 64 : (i + 1) * 64]
            return 0

        lax.fori_loop(0, NX, block, 0)
        for r in blocks:
            hand_over(r)

    def hand_over(r):
        target = (z + NZ - r) % NZ

        @pl.when(target != tp)
        def _():
            block_copy(r).start()

        @pl.when(target == tp)
        def _():
            rbuf[tp] = part[r]

    project(0)
    for j in (1, 2, 3, 4):
        for s in range(2):
            for d in range(2):
                if j < 4 or s == d:
                    a_copy(s, d, j).wait_recv()
                if j < 3 or (j == 3 and s == d):
                    a_start(s, d, j + 1)
        project(*((j, 8 - j) if j < 4 else (j,)))

    total = jnp.zeros((64, 1024), F32)
    for t in range(NT):

        @pl.when(t != tp)
        def _():
            remote(part.at[0], rbuf.at[t], r_send.at[0], r_recv.at[t], t_to[1]).wait_recv()

    for t in range(NT):
        total = total + rbuf[t].astype(F32)
    total = total.astype(BF)
    rows = pl.ds(pl.multiple_of(x * 64, 64), 64)
    fin[rows, :] = total[:, 0:256]
    for k in range(1, NX):
        fin_s[k - 1] = total[:, k * 256 : (k + 1) * 256]
        cp = remote(fin_s.at[k - 1], fin.at[rows], f_send.at[k - 1], f_recv.at[k - 1], x_to[k])
        cp.start()
        sent.append(cp)
    for k in range(1, NX):
        from_rows = pl.ds(pl.multiple_of(((x + NX - k) % NX) * 64, 64), 64)
        remote(fin_s.at[k - 1], fin.at[from_rows], f_send.at[k - 1], f_recv.at[k - 1], x_to[k]).wait_recv()
    lo_ref[...] = fin[...]
    for r in range(NZ):

        @pl.when((z + NZ - r) % NZ != tp)
        def _():
            block_copy(r).wait_send()

    for cp in sent:
        cp.wait_send()
    for cp in flush:
        cp.wait()


def handoff(level, t3, t12, lens, q, nk, nv, key_pool, value_pool, out_weight):
    caps = LEVELS[level]
    n = len(CHUNKS)
    smem = pl.BlockSpec(memory_space=pltpu.SMEM)
    vmem = pl.BlockSpec(memory_space=pltpu.VMEM)
    hbm = pl.BlockSpec(memory_space=pl.ANY)
    dma = pltpu.SemaphoreType.DMA
    scratch = [pltpu.VMEM((POOL, PAGE, HD), BF)] * 2 + [pltpu.VMEM((2, SPAN, HD), BF)] * 2
    for pages in ((2 * SEND_MINUS,), ZROOM, (3 * XFULL,), (4 * XFULL,)):
        scratch += [pltpu.VMEM((k, rows, HD), BF) for _, _, rows in CHUNKS for k in pages]
    scratch += [
        pltpu.VMEM((2, 256, SPAN), BF),
        pltpu.VMEM((2, 2, 256, 128), F32),
        pltpu.VMEM((NX, 1024, 256), BF),
        pltpu.VMEM((NZ, 64, 1024), BF),
        pltpu.VMEM((NZ, 64, 1024), BF),
        pltpu.VMEM((NT, 64, 1024), BF),
        pltpu.VMEM((3, 64, 256), BF),
        pltpu.VMEM((256, 256), BF),
        dma((5,)),
        dma((n, 2, 4)),
        dma((n, 2, 4)),
        dma((n, 2, 3)),
        dma((n, 2, 3)),
        dma((4,)),
        dma((4,)),
        dma((2, 2, 4)),
        dma((2, 2, 4)),
        dma((NZ,)),
        dma((NT,)),
        dma((3,)),
        dma((3,)),
    ]
    return pl.pallas_call(
        functools.partial(handoff_kernel, caps),
        out_shape=(
            jax.ShapeDtypeStruct((256, 256), BF),
            jax.ShapeDtypeStruct((2, SPAN, HD), BF),
            jax.ShapeDtypeStruct((2, SPAN, HD), BF),
        ),
        in_specs=[smem] * 3 + [vmem] * 3 + [hbm] * 3,
        out_specs=(vmem, hbm, hbm),
        scratch_shapes=scratch,
        compiler_params=pltpu.CompilerParams(
            collective_id=level, has_side_effects=True, vmem_limit_bytes=58 * 2**20
        ),
    )(t3, t12, lens, q, nk, nv, key_pool, value_pool, out_weight)


def local(queries, new_keys, new_values, key_pool, value_pool, out_weight, mem_len, assign, block_table):
    t3, t12, lens, level = make_tables(mem_len, assign, block_table)
    q = queries.reshape(64, 1024)
    nk = new_keys.reshape(64, HD)
    nv = new_values.reshape(64, HD)
    branches = [functools.partial(handoff, i) for i in range(len(LEVELS))]
    return lax.switch(level[0], branches, t3, t12, lens, q, nk, nv, key_pool, value_pool, out_weight)


def solution(mesh):
    placed = (
        P("dp", None, None, "tp"),
        P("dp", None, None, "tp"),
        P("dp", None, None, "tp"),
        P("dp", None, "tp"),
        P("dp", None, "tp"),
        P("tp", "dp"),
        P(),
        P(),
        P(),
    )
    return jax.shard_map(
        local,
        mesh=mesh,
        in_specs=placed,
        out_specs=(P("tp", "dp"), P("dp", None, "tp"), P("dp", None, "tp")),
        check_vma=False,
    )
```

```python
import functools
import math

import jax
import jax.numpy as jnp
from jax import lax
from jax.experimental import pallas as pl
from jax.experimental.pallas import tpu as pltpu
from jax.sharding import PartitionSpec as P

MESH = pl.DeviceIdType.MESH
BF = jnp.bfloat16
F32 = jnp.float32
I32 = jnp.int32

NZ, NX, NT = 8, 4, 8
HD = 128
QPK = 8
PAGE = 64
PAGES = 80
POOL = 160
SPAN = PAGES * PAGE

FULL = (73, 53, 33, 13)
XFULL = 40
LEVELS = (
    (36, 28, 19, 9),
    (39, 30, 21, 10),
    (45, 34, 24, 12),
    FULL,
)
OWN = 20
PLUS = (20, 93, 0, 33)
MINUS = (146, 219, 46, 79)
ZROOM = (272, 92)
XNEAR = 25
SEND_MINUS = FULL[0]
LIST = 168
CHUNKS = tuple((w, r, 16) for w in (0, 1) for r in (0, 16, 32, 48))


def dot(a, b, dims, precision=None):
    return lax.dot_general(a, b, (dims, ((), ())), precision=precision, preferred_element_type=F32)


def tables_kernel(len_ref, assign_ref, bt_ref, t3_ref, t12_ref, lens_ref, level_ref, raw, longs, src_s, used_s, list_s):
    me = lax.axis_index("dp")
    z, x = me // NX, me % NX
    raw[...] = jnp.zeros_like(raw)
    for s in range(64):
        a = assign_ref[s]
        raw[s : s + 1, 0:PAGES] = bt_ref[pl.ds(a, 1), :]
        longs[s : s + 1, :] = jnp.full((1, 128), len_ref[a], I32)

    shape = (64, 128)
    slot = lax.broadcasted_iota(I32, shape, 0)
    lane = lax.broadcasted_iota(I32, shape, 1)
    page = raw[...]
    src = (page * 26215) >> 22
    loc = (page - src * POOL).astype(F32)
    used = jnp.where((lane < PAGES) & (lane * PAGE < longs[...]), 1, 0)
    src = jnp.where(used == 1, src, 1000)
    src_s[...] = src

    tri = jnp.where(lax.broadcasted_iota(I32, (128, 128), 0) < lax.broadcasted_iota(I32, (128, 128), 1), 1.0, 0.0).astype(BF)
    bi, bj = lax.broadcasted_iota(I32, (64, 64), 0), lax.broadcasted_iota(I32, (64, 64), 1)
    blocks = jnp.where((bi // 8 == bj // 8) & (bj < bi), 1.0, 0.0).astype(BF)

    def ranks(mask):
        total = jnp.broadcast_to(jnp.sum(mask, axis=1, keepdims=True), shape)
        return dot(mask.astype(BF), tri, ((1,), (0,))) + dot(blocks, total.astype(BF), ((1,), (0,)))

    count = jnp.zeros(shape, F32)
    for e in range(32):
        total = jnp.sum(jnp.where(src == e, 1.0, 0.0), axis=1, keepdims=True)
        count = jnp.where(lane == e, total, count)
    dist = (slot // 8 - lane // NX) & 7
    at = [jnp.sum(jnp.where((dist == k) & (lane < 32), count, 0.0), axis=0, keepdims=True) for k in range(8)]
    lean = (at[5] + at[6] + at[7] - at[1] - at[2] - at[3]) * 0.25
    middle = at[4] * 0.5
    p4 = jnp.clip(
        jnp.floor(middle + lean + 0.5),
        jnp.floor(jnp.maximum(middle - 3.0, 0.0)),
        jnp.minimum(at[4], jnp.ceil(middle) + 3.0),
    )
    m4 = at[4] - p4
    plus = [None] * 5
    minus = [None] * 5
    plus[4], minus[4] = p4, m4
    for j in (3, 2, 1):
        plus[j] = plus[j + 1] + at[j]
        minus[j] = minus[j + 1] + at[8 - j]
    nil = jnp.zeros_like(p4)
    offset = [nil, plus[2], plus[3], plus[4], nil, minus[4], minus[3], minus[2]]

    needs = [(jnp.maximum(jnp.max(plus[j]), jnp.max(minus[j])), j - 1) for j in (1, 2, 3, 4)]
    level = jnp.int32(0)
    for caps in LEVELS[:-1]:
        over = jnp.int32(0)
        for need, j in needs:
            over = jnp.maximum(over, jnp.where(need > float(caps[j]), 1, 0))
        level = level + over
    level_ref[0] = level

    def column(row, e):
        return jnp.sum(jnp.where(lax.broadcasted_iota(I32, (1, 128), 1) == e, row, 0.0), axis=1, keepdims=True)

    mine = src == me
    rank = ranks(jnp.where(mine, 1.0, 0.0))
    away = (slot // 8 - z) & 7
    half = column(p4, me)
    place = rank
    for k in range(1, 8):
        base = OWN if k < 4 else OWN + SEND_MINUS
        value = column(offset[k], me) + rank + float(base)
        if k == 4:
            value = jnp.where(rank < half, rank + float(OWN), rank - half + float(OWN + SEND_MINUS))
        place = jnp.where(away == k, value, place)
    place = jnp.where(mine, place, -1.0)

    def first_list(g, _):
        rows = []
        for i in range(8):
            k = (g * 8 + i).astype(F32)
            rows.append(jnp.sum(jnp.where(place == k, loc, 0.0), axis=0, keepdims=True))
        list_s[pl.ds(pl.multiple_of(g * 8, 8), 8), :] = jnp.concatenate(rows, axis=0)
        return 0

    lax.fori_loop(0, LIST // 8, first_list, 0)
    ones = jnp.ones((8, 128), F32)
    t12_ref[0:8, :] = dot(ones, list_s[...], ((1,), (1,)), lax.Precision.HIGHEST).astype(I32)

    row8 = pl.ds(pl.multiple_of(z * 8, 8), 8)
    src_r = src_s[row8, :]
    marks = jnp.concatenate([jnp.where(src_r == zs * NX + x, 1.0, 0.0) for zs in range(NZ)], axis=0)
    rank = ranks(marks)
    off8 = jnp.concatenate(offset, axis=0)
    k8 = lax.broadcasted_iota(I32, (8, 128), 0)
    e8 = lax.broadcasted_iota(I32, (8, 128), 1)
    here = (e8 & 3) == x
    off_e = jnp.sum(jnp.where(here & (k8 == ((z - e8 // NX) & 7)), off8, 0.0), axis=0, keepdims=True)
    half_e = jnp.where(here[0:1], p4, 0.0)
    through = jnp.zeros((8, 128), F32)
    for zs in range(NZ):
        r = rank[zs * 8 : zs * 8 + 8]
        pick = (e8[0:1] // NX) == zs
        off = jnp.sum(jnp.where(pick, off_e, 0.0), axis=1, keepdims=True)
        half = jnp.sum(jnp.where(pick, half_e, 0.0), axis=1, keepdims=True)
        d = jnp.broadcast_to((z - zs) & 7, (8, 128))
        value = r
        for k in range(1, 8):
            if k == 4:
                v = jnp.where(r < half, r + float(PLUS[3]), r - half + float(MINUS[3]))
            else:
                v = off + r + float(PLUS[k - 1] if k < 4 else MINUS[7 - k])
            value = jnp.where(d == k, v, value)
        through = through + marks[zs * 8 : zs * 8 + 8] * value

    used_r = src_r < 32
    odd = (k8 & 1) == 1
    apart = (z - (src_r >> 2)) & 7
    far = (apart >= 3) & (apart <= 5)
    order = jnp.where(far, float(XNEAR), 0.0)
    for k in range(2 * NX):
        mark = jnp.where(used_r & ((src_r & 3) == k // 2) & (far if k % 2 else ~far), 1.0, 0.0)
        total = jnp.broadcast_to(jnp.sum(mark, axis=1, keepdims=True), (8, 128))
        r = dot(mark.astype(BF), tri, ((1,), (0,))) + jnp.where(odd, pltpu.roll(total, 1, 0), 0.0)
        order = order + mark * r
    order_i = order.astype(I32)
    t3_ref[...] = jnp.where(used_r, ((src_r - x) & 3) * XFULL + order_i, 0)
    lens_ref[...] = longs[row8, :]
    goes = ((k8 // 2 - x) & 3) * XFULL + order_i
    goes = jnp.where(used_r & ((src_r & 3) == x), goes, -1)

    def second_list(g, _):
        rows = []
        for i in range(8):
            rows.append(jnp.sum(jnp.where(goes == g * 8 + i, through, 0.0), axis=0, keepdims=True))
        list_s[pl.ds(pl.multiple_of(g * 8, 8), 8), :] = jnp.concatenate(rows, axis=0)
        return 0

    lax.fori_loop(0, LIST // 8, second_list, 0)
    t12_ref[8:16, :] = dot(ones, list_s[...], ((1,), (1,)), lax.Precision.HIGHEST).astype(I32)


def make_tables(mem_len, assign, block_table):
    smem = pl.BlockSpec(memory_space=pltpu.SMEM)
    vmem = pl.BlockSpec(memory_space=pltpu.VMEM)
    return pl.pallas_call(
        tables_kernel,
        out_shape=(
            jax.ShapeDtypeStruct((8, 128), I32),
            jax.ShapeDtypeStruct((16, LIST), I32),
            jax.ShapeDtypeStruct((8, 128), I32),
            jax.ShapeDtypeStruct((1,), I32),
        ),
        in_specs=[smem, smem, vmem],
        out_specs=(vmem, vmem, vmem, smem),
        scratch_shapes=[
            pltpu.VMEM((64, 128), I32),
            pltpu.VMEM((64, 128), I32),
            pltpu.VMEM((64, 128), I32),
            pltpu.VMEM((64, 128), I32),
            pltpu.VMEM((LIST, 128), F32),
        ],
    )(mem_len, assign, block_table)


def handoff_kernel(caps, *refs):
    n = len(CHUNKS)
    it = iter(refs)
    t3, t12, lens, q_ref, nk_ref, nv_ref, kp_hbm, vp_hbm, w_hbm = (next(it) for _ in range(9))
    lo_ref, ko_hbm, vo_hbm = (next(it) for _ in range(3))
    pools = (next(it), next(it))
    staged = (next(it), next(it))
    zs = [next(it) for _ in range(n)]
    zb = [(next(it), next(it)) for _ in range(n)]
    xs = [next(it) for _ in range(n)]
    xb = [next(it) for _ in range(n)]
    seq, probs, att, wbuf, abuf, part, rbuf, fin_s, fin = (next(it) for _ in range(9))
    local_sem, z_send, z_recv, x_send, x_recv, w_send, w_recv, a_send, a_recv, r_send, r_recv, f_send, f_recv = it

    me, tp = lax.axis_index("dp"), lax.axis_index("tp")
    z, x = me // NX, me % NX
    z_to = [{"dp": ((z + 1) % NZ) * NX + x}, {"dp": ((z + NZ - 1) % NZ) * NX + x}]
    x_to = [{"dp": z * NX + (x + r) % NX} for r in range(NX)]
    t_to = [{"tp": (tp + r) % NT} for r in range(NT)]

    loads = [
        pltpu.make_async_copy(kp_hbm, pools[0], local_sem.at[0]),
        pltpu.make_async_copy(vp_hbm, pools[1], local_sem.at[1]),
        pltpu.make_async_copy(w_hbm, wbuf.at[0], local_sem.at[2]),
    ]
    for c in loads:
        c.start()
    barrier = pltpu.get_barrier_semaphore()
    peers = z_to + x_to[1:] + t_to[1:]
    for d in peers:
        pl.semaphore_signal(barrier, inc=1, device_id=d, device_id_type=MESH)

    def remote(src, dst, ss, rs, to):
        return pltpu.make_async_remote_copy(
            src_ref=src, dst_ref=dst, send_sem=ss, recv_sem=rs, device_id=to, device_id_type=MESH
        )

    sent = []

    def z_copy(c, d, j):
        base = (PLUS, MINUS)[d]
        if j == 1:
            src = zs[c].at[pl.ds(d * SEND_MINUS, caps[0])]
        else:
            src = zb[c][(j - 2) // 2].at[pl.ds(base[j - 2], caps[j - 1])]
        dst = zb[c][(j - 1) // 2].at[pl.ds(base[j - 1], caps[j - 1])]
        return remote(src, dst, z_send.at[c, d, j - 1], z_recv.at[c, d, j - 1], z_to[d])

    def z_start(c, j):
        for d in range(2):
            cp = z_copy(c, d, j)
            cp.start()
            sent.append(cp)

    spans = ((0, XNEAR), (XNEAR, XFULL - XNEAR))

    def x_copy(c, r, far):
        first, pages = spans[far]
        return remote(
            xs[c].at[pl.ds((r - 1) * XFULL + first, pages)],
            xb[c].at[pl.ds((NX - r) * XFULL + first, pages)],
            x_send.at[c, far, r - 1],
            x_recv.at[c, far, r - 1],
            x_to[r],
        )

    def pack_pool(which):
        mine = [(c, r0, rows) for c, (w, r0, rows) in enumerate(CHUNKS) if w == which]
        pool = pools[which]

        def body(first, dst, place, k, _):
            got = pool[t12[0, first + k]]
            for c, r0, rows in mine:
                dst[c][place + k] = got[r0 : r0 + rows]
            return 0

        near = [z[0] for z in zb]

        lax.fori_loop(0, OWN, functools.partial(body, 0, near, 0), 0, unroll=4)
        lax.fori_loop(0, caps[0], functools.partial(body, OWN, zs, 0), 0, unroll=2)
        lax.fori_loop(0, caps[0], functools.partial(body, OWN + SEND_MINUS, zs, SEND_MINUS), 0, unroll=2)

    def pack_row(c, far):
        start, pages = spans[far]

        def body(first, dst, place, k, _):
            dst[place + k] = zb[c][far][t12[8, first + k]]
            return 0

        for r in (2, 1, 3):
            put = functools.partial(body, r * XFULL + start, xs[c], (r - 1) * XFULL + start)
            lax.fori_loop(0, pages, put, 0, unroll=5)
            cp = x_copy(c, r, far)
            cp.start()
            sent.append(cp)
        lax.fori_loop(0, pages, functools.partial(body, start, xb[c], start), 0, unroll=5)

    def place_pages(c):
        which, r0, rows = CHUNKS[c]
        token = lax.broadcasted_iota(I32, (rows, HD), 0)
        def slot(s, _):
            length = lens[2 * x + s, 0] - r0

            def body(p, _):
                got = xb[c][t3[2 * x + s, p]]
                got = jnp.where(token < length - p * PAGE, got.astype(F32), 0.0).astype(BF)
                staged[which][s, pl.ds(pl.multiple_of(p * PAGE + r0, 16), rows), :] = got
                seq[c, s, pl.ds(pl.multiple_of(p * rows, 16), rows), :] = got
                return 0

            return lax.fori_loop(0, PAGES, body, 0, unroll=4)

        lax.fori_loop(0, 2, slot, 0)

    scale = 1.0 / math.sqrt(HD)
    tile = 640
    span = SPAN // 4

    def slot_rows(s):
        return pl.ds(pl.multiple_of(s * 32, 32), 32)

    def queries_of(s):
        rows = q_ref[slot_rows(s), :]
        return jnp.concatenate([rows[:, h * HD : (h + 1) * HD] for h in range(QPK)], axis=0)

    def fresh_scores(s):
        sc = dot(queries_of(s), nk_ref[slot_rows(s), :], ((1,), (1,))) * scale
        r = lax.broadcasted_iota(I32, sc.shape, 0) % 32
        u = lax.broadcasted_iota(I32, sc.shape, 1)
        ok = (r // 4 == u // 4) & (u % 4 <= r % 4)
        return jnp.where(ok, sc, -jnp.inf)

    def tile_scores(s, q, c, i, length):
        keys = seq[c, s, pl.ds(pl.multiple_of(i * tile, 128), tile), :]
        sc = dot(q, keys, ((1,), (1,))) * scale
        at = lax.broadcasted_iota(I32, sc.shape, 1) + i * tile
        pos = (at >> 4) * PAGE + (at & 15) + c * 16
        return jnp.where(pos < length, sc, -jnp.inf)

    def find_max(s):
        q = queries_of(s)
        length = lens[2 * x + s, 0]

        def body(i, m):
            sc = tile_scores(s, q, i >> 1, i & 1, length)
            for k in range(tile // 128):
                m = jnp.maximum(m, sc[:, k * 128 : (k + 1) * 128])
            return m

        att[s, 0] = lax.fori_loop(0, SPAN // tile, body, jnp.full((256, 128), -jnp.inf, F32))

    def weigh(s):
        q = queries_of(s)
        length = lens[2 * x + s, 0]
        last = fresh_scores(s)
        top = jnp.maximum(jnp.max(att[s, 0], axis=1, keepdims=True), jnp.max(last, axis=1, keepdims=True))

        def body(i, t):
            w = jnp.exp(tile_scores(s, q, i >> 1, i & 1, length) - top)
            probs[s, :, pl.ds(pl.multiple_of(i * tile, 128), tile)] = w.astype(BF)
            for k in range(tile // 128):
                t = t + w[:, k * 128 : (k + 1) * 128]
            return t

        t = lax.fori_loop(0, SPAN // tile, body, jnp.zeros((256, 128), F32))
        fresh = jnp.exp(last - top)
        total = jnp.sum(t, axis=1, keepdims=True) + jnp.sum(fresh, axis=1, keepdims=True)
        att[s, 0] = jnp.broadcast_to(total, (256, 128))
        att[s, 1] = dot(fresh.astype(BF), nv_ref[slot_rows(s), :], ((1,), (0,)))

    def add_values(s, first, last):
        def body(c, a):
            at = pl.ds(pl.multiple_of(c * span, 128), span)
            return a + dot(probs[s, :, at], seq[c + 4, s], ((1,), (0,)))

        att[s, 1] = lax.fori_loop(first, last, body, att[s, 1])

    def finish(s):
        add_values(s, 3, 4)
        rows = (att[s, 1] / att[s, 0]).astype(BF)
        for h in range(QPK):
            abuf[0, slot_rows(s), h * HD : (h + 1) * HD] = rows[h * 32 : (h + 1) * 32, :]

    half = wbuf.shape[1] // 2

    def w_copy(i):
        src, dst, r = (
            (wbuf.at[0], wbuf.at[3], 1),
            (wbuf.at[0], wbuf.at[1], 3),
            (wbuf.at[3, pl.ds(0, half)], wbuf.at[2, pl.ds(0, half)], 1),
            (wbuf.at[1, pl.ds(half, half)], wbuf.at[2, pl.ds(half, half)], 3),
        )[i]
        return remote(src, dst, w_send.at[i], w_recv.at[i], x_to[r])

    def w_start(i):
        cp = w_copy(i)
        cp.start()
        sent.append(cp)

    pl.semaphore_wait(barrier, len(peers))
    loads[0].wait()
    pack_pool(0)
    z_start(0, 1)
    z_start(1, 1)
    loads[2].wait()
    w_start(0)
    w_start(1)
    loads[1].wait()
    pack_pool(1)

    k_last = max(c for c, ch in enumerate(CHUNKS) if ch[0] == 0)
    def both(f):
        def body(s, _):
            f(s)
            return 0

        lax.fori_loop(0, 2, body, 0)

    flush = []
    for r in range(1, n + 5):
        for c in range(max(0, r - 4), min(n, r)):
            j = r - c
            for d in range(2):
                z_copy(c, d, j).wait_recv()
            if j < 4:
                z_start(c, j + 1)
        if r + 1 < n:
            z_start(r + 1, 1)
        if r == 2:
            w_copy(0).wait_recv()
            w_copy(1).wait_recv()
            w_start(2)
            w_start(3)
        if 0 <= r - 4 < n:
            pack_row(r - 4, 1)
        if 0 <= r - 2 < n:
            pack_row(r - 2, 0)
        if 0 <= r - 5 < n:
            c = r - 5
            for far in range(2):
                for i in (1, 2, 3):
                    x_copy(c, i, far).wait_recv()
            place_pages(c)
            if c == k_last:
                out = pltpu.make_async_copy(staged[0], ko_hbm, local_sem.at[3])
                out.start()
                flush.append(out)
        if r == n:
            both(find_max)
        if r == n + 1:
            both(weigh)
        if r == n + 3:
            both(functools.partial(add_values, first=0, last=3))
    out = pltpu.make_async_copy(staged[1], vo_hbm, local_sem.at[4])
    out.start()
    flush.append(out)

    def a_copy(s, d, j):
        rows = pl.ds(s * 32, 32)
        here = (j - 1) if d == 0 else (9 - j) % 8
        there = j if d == 0 else 8 - j
        return remote(abuf.at[here, rows], abuf.at[there, rows], a_send.at[s, d, j - 1], a_recv.at[s, d, j - 1], z_to[d])

    def a_start(s, d, j):
        cp = a_copy(s, d, j)
        cp.start()
        sent.append(cp)

    for s in range(2):
        finish(s)
        for d in range(2):
            a_start(s, d, 1)

    w_copy(2).wait_recv()
    w_copy(3).wait_recv()

    def block_copy(r):
        return remote(part.at[r], rbuf.at[tp], r_send.at[r], r_recv.at[tp], {"tp": (z + NZ - r) % NZ})

    def project(*blocks):
        rows = jnp.concatenate([abuf[r] for r in blocks], axis=0) if len(blocks) > 1 else abuf[blocks[0]]

        def block(k, _):
            columns = pl.ds(pl.multiple_of(k * 256, 256), 256)
            got = dot(rows, wbuf[k], ((1,), (0,))).astype(BF)
            for i, r in enumerate(blocks):
                part[r, :, columns] = got[i * 64 : (i + 1) * 64]
            return 0

        lax.fori_loop(0, NX, block, 0)
        for r in blocks:
            hand_over(r)

    def hand_over(r):
        target = (z + NZ - r) % NZ

        @pl.when(target != tp)
        def _():
            block_copy(r).start()

        @pl.when(target == tp)
        def _():
            rbuf[tp] = part[r]

    project(0)
    for j in (1, 2, 3, 4):
        for s in range(2):
            for d in range(2):
                if j < 4 or s == d:
                    a_copy(s, d, j).wait_recv()
                if j < 3 or (j == 3 and s == d):
                    a_start(s, d, j + 1)
        project(*((j, 8 - j) if j < 4 else (j,)))

    total = jnp.zeros((64, 1024), F32)
    for t in range(NT):

        @pl.when(t != tp)
        def _():
            remote(part.at[0], rbuf.at[t], r_send.at[0], r_recv.at[t], t_to[1]).wait_recv()

    for t in range(NT):
        total = total + rbuf[t].astype(F32)
    total = total.astype(BF)
    rows = pl.ds(pl.multiple_of(x * 64, 64), 64)
    fin[rows, :] = total[:, 0:256]
    for k in range(1, NX):
        fin_s[k - 1] = total[:, k * 256 : (k + 1) * 256]
        cp = remote(fin_s.at[k - 1], fin.at[rows], f_send.at[k - 1], f_recv.at[k - 1], x_to[k])
        cp.start()
        sent.append(cp)
    for k in range(1, NX):
        from_rows = pl.ds(pl.multiple_of(((x + NX - k) % NX) * 64, 64), 64)
        remote(fin_s.at[k - 1], fin.at[from_rows], f_send.at[k - 1], f_recv.at[k - 1], x_to[k]).wait_recv()
    lo_ref[...] = fin[...]
    for r in range(NZ):

        @pl.when((z + NZ - r) % NZ != tp)
        def _():
            block_copy(r).wait_send()

    for cp in sent:
        cp.wait_send()
    for cp in flush:
        cp.wait()


def handoff(level, t3, t12, lens, q, nk, nv, key_pool, value_pool, out_weight):
    caps = LEVELS[level]
    n = len(CHUNKS)
    smem = pl.BlockSpec(memory_space=pltpu.SMEM)
    vmem = pl.BlockSpec(memory_space=pltpu.VMEM)
    hbm = pl.BlockSpec(memory_space=pl.ANY)
    dma = pltpu.SemaphoreType.DMA
    scratch = [pltpu.VMEM((POOL, PAGE, HD), BF)] * 2 + [pltpu.VMEM((2, SPAN, HD), BF)] * 2
    for pages in ((2 * SEND_MINUS,), ZROOM, (3 * XFULL,), (4 * XFULL,)):
        scratch += [pltpu.VMEM((k, rows, HD), BF) for _, _, rows in CHUNKS for k in pages]
    scratch += [
        pltpu.VMEM((n, 2, SPAN // 4, HD), BF),
        pltpu.VMEM((2, 256, SPAN), BF),
        pltpu.VMEM((2, 2, 256, 128), F32),
        pltpu.VMEM((NX, 1024, 256), BF),
        pltpu.VMEM((NZ, 64, 1024), BF),
        pltpu.VMEM((NZ, 64, 1024), BF),
        pltpu.VMEM((NT, 64, 1024), BF),
        pltpu.VMEM((3, 64, 256), BF),
        pltpu.VMEM((256, 256), BF),
        dma((5,)),
        dma((n, 2, 4)),
        dma((n, 2, 4)),
        dma((n, 2, 3)),
        dma((n, 2, 3)),
        dma((4,)),
        dma((4,)),
        dma((2, 2, 4)),
        dma((2, 2, 4)),
        dma((NZ,)),
        dma((NT,)),
        dma((3,)),
        dma((3,)),
    ]
    return pl.pallas_call(
        functools.partial(handoff_kernel, caps),
        out_shape=(
            jax.ShapeDtypeStruct((256, 256), BF),
            jax.ShapeDtypeStruct((2, SPAN, HD), BF),
            jax.ShapeDtypeStruct((2, SPAN, HD), BF),
        ),
        in_specs=[smem] * 3 + [vmem] * 3 + [hbm] * 3,
        out_specs=(vmem, hbm, hbm),
        scratch_shapes=scratch,
        compiler_params=pltpu.CompilerParams(
            collective_id=level, has_side_effects=True, vmem_limit_bytes=58 * 2**20
        ),
    )(t3, t12, lens, q, nk, nv, key_pool, value_pool, out_weight)


def local(queries, new_keys, new_values, key_pool, value_pool, out_weight, mem_len, assign, block_table):
    t3, t12, lens, level = make_tables(mem_len, assign, block_table)
    q = queries.reshape(64, 1024)
    nk = new_keys.reshape(64, HD)
    nv = new_values.reshape(64, HD)
    branches = [functools.partial(handoff, i) for i in range(len(LEVELS))]
    return lax.switch(level[0], branches, t3, t12, lens, q, nk, nv, key_pool, value_pool, out_weight)


def solution(mesh):
    placed = (
        P("dp", None, None, "tp"),
        P("dp", None, None, "tp"),
        P("dp", None, None, "tp"),
        P("dp", None, "tp"),
        P("dp", None, "tp"),
        P("tp", "dp"),
        P(),
        P(),
        P(),
    )
    return jax.shard_map(
        local,
        mesh=mesh,
        in_specs=placed,
        out_specs=(P("tp", "dp"), P("dp", None, "tp"), P("dp", None, "tp")),
        check_vma=False,
    )
```
